256 devices in a mesh: gx: 8 (over z), gy: 8 (over y, core), gz: 4 (over x).
Axes of the slice: x: 4, y: 4, z: 8, core: 2. Of those that a mesh axis runs over, the one named last changes fastest.
Arguments:
- source_term: float32 [128, 256, 512], P('gx', 'gy', 'gz'), may hold values from -9 to 9
- alpha_cell: float32 [128, 256, 512], P('gx', 'gy', 'gz'), may hold values from 0.5 to 2
- beta_x: float32 [128, 256, 512], P('gx', 'gy', 'gz'), may hold values from 4 to 40
- beta_y: float32 [128, 256, 512], P('gx', 'gy', 'gz'), may hold values from 4 to 40
- beta_z: float32 [128, 256, 512], P('gx', 'gy', 'gz'), may hold values from 4 to 40
Outputs:
- iterate_fine: float32 [128, 256, 512], P('gx', 'gy', 'gz')
- iterate_one: float32 [64, 128, 256], P('gx', 'gy', 'gz')
- iterate_two: float32 [32, 64, 128], P('gx', 'gy', 'gz')
- iterate_three: float32 [16, 32, 64], P('gx', 'gy', 'gz')
- bottom_source: float32 [8, 16, 32], replicated
The draws below stay inside these ranges and needn't reach their ends.
All inputs are finite; a program needn't handle non-finite values.
Results may differ from the reference program's by a relative error of at most 0.00011.
Values sent between devices are 32-bit elements; how exact they have to be, the bound alone decides.
A program may use at most 128 MiB of HBM per device.

```python
import math
import jax
import jax.numpy as jnp

LEVELS = 4
SWEEPS = 4
NX = 128
NY = 256
NZ = 512


def draw_source_term(key, part):
    key = jax.random.fold_in(key, 11)
    noise_key, mode_key = jax.random.split(key, 2)
    mode_numbers = jax.random.randint(mode_key, (3,), 1, 4).astype(jnp.float32)
    coord_x = (jnp.arange(NX, dtype=jnp.float32) + 0.5) / NX
    coord_y = (jnp.arange(NY, dtype=jnp.float32) + 0.5) / NY
    coord_z = (jnp.arange(NZ, dtype=jnp.float32) + 0.5) / NZ
    wave_x = jnp.sin(math.pi * mode_numbers[0] * coord_x)
    wave_y = jnp.sin(math.pi * mode_numbers[1] * coord_y)
    wave_z = jnp.sin(math.pi * mode_numbers[2] * coord_z)
    modal_part = wave_x[:, None, None] * wave_y[None, :, None] * wave_z[None, None, :]
    rough_part = jnp.clip(jax.random.normal(noise_key, (NX, NY, NZ), jnp.float32), -4.0, 4.0)
    smooth_part = 3.0 * modal_part
    return rough_part + smooth_part


def shard_levels(rng, extent, shards, smallest, top_value):
    loudness, own = 1.0, jax.random.fold_in(rng, 6)
    for dim, shards_of in shards:
        heights = jnp.exp(jax.random.uniform(jax.random.fold_in(own, dim), (shards_of,), jnp.float32, smallest / len(shards), top_value / len(shards)))
        loudness = loudness * jnp.repeat(heights, extent[dim] // shards_of).reshape([-1 if axis == dim else 1 for axis in range(len(extent))])
    return loudness


def setup_inputs(seed: int = 0) -> dict:
    key_of = jax.random.split(jax.random.key(seed), 6)
    source_term = draw_source_term(jax.random.fold_in(key_of[5], 71), 0)
    alpha_cell = jnp.clip(jnp.exp(math.log(2.0) - 1.3862944 * jax.random.uniform(key_of[1], (NX, NY, NZ), jnp.float32) ** shard_levels(key_of[1], (NX, NY, NZ), ((0, 8), (1, 8), (2, 4)), -0.2, 0.2)), 0.5, 2.0)
    beta_x = jnp.clip(jnp.exp(math.log(40.0) - 2.3025851 * jax.random.uniform(key_of[2], (NX, NY, NZ), jnp.float32) ** shard_levels(key_of[2], (NX, NY, NZ), ((0, 8), (1, 8), (2, 4)), -0.2, 0.2)), 4.0, 40.0)
    beta_y = jnp.clip(jnp.exp(math.log(40.0) - 2.3025851 * jax.random.uniform(key_of[3], (NX, NY, NZ), jnp.float32) ** shard_levels(key_of[3], (NX, NY, NZ), ((0, 8), (1, 8), (2, 4)), -0.2, 0.2)), 4.0, 40.0)
    beta_z = jnp.clip(jnp.exp(math.log(40.0) - 2.3025851 * jax.random.uniform(key_of[4], (NX, NY, NZ), jnp.float32) ** shard_levels(key_of[4], (NX, NY, NZ), ((0, 8), (1, 8), (2, 4)), -0.2, 0.2)), 4.0, 40.0)
    return dict(source_term=source_term, alpha_cell=alpha_cell, beta_x=beta_x, beta_y=beta_y, beta_z=beta_z)


spectrum_low = 0.25
spectrum_high = 2.0


def chebyshev_weights(count):
    middle = 0.5 * (spectrum_high + spectrum_low)
    spread = 0.5 * (spectrum_high - spectrum_low)
    sharpness = middle / spread
    weights = [(0.0, 1.0 / middle)]
    rho_prev = 1.0 / sharpness
    for sweep_index in range(1, count):
        rho_next = 1.0 / (2.0 * sharpness - rho_prev)
        weights.append((rho_next * rho_prev, 2.0 * rho_next / spread))
        rho_prev = rho_next
    return weights


def interior(field_values):
    return field_values[1:-1, 1:-1, 1:-1]


def neighbours(current, face_betas):
    face_x, face_y, face_z = face_betas
    summed = interior(face_x) * current[:-2, 1:-1, 1:-1] + face_x[2:, 1:-1, 1:-1] * current[2:, 1:-1, 1:-1]
    summed = summed + (interior(face_y) * current[1:-1, :-2, 1:-1] + face_y[1:-1, 2:, 1:-1] * current[1:-1, 2:, 1:-1])
    summed = summed + (interior(face_z) * current[1:-1, 1:-1, :-2] + face_z[1:-1, 1:-1, 2:] * current[1:-1, 1:-1, 2:])
    return summed


def diagonal(alpha_values, face_betas, level_scale):
    face_x, face_y, face_z = face_betas
    face_sum = (interior(face_x) + face_x[2:, 1:-1, 1:-1]) + (interior(face_y) + face_y[1:-1, 2:, 1:-1])
    face_sum = face_sum + (interior(face_z) + face_z[1:-1, 1:-1, 2:])
    return alpha_values + level_scale * face_sum


def apply_operator(current, face_betas, center_weight, level_scale):
    return center_weight * interior(current) - level_scale * neighbours(current, face_betas)


def chebyshev_sweep(current, older, face_betas, source, center_weight, inverse, level_scale, momentum, step_weight):
    middle = interior(current)
    update = source - apply_operator(current, face_betas, center_weight, level_scale)
    return middle + momentum * (middle - older) + step_weight * inverse * update


def pad_one(field_values):
    return jnp.pad(field_values, 1)


def smooth_level(source, alpha_values, face_betas, level_scale):
    padded_betas = tuple(pad_one(face_values) for face_values in face_betas)
    center_weight = diagonal(alpha_values, padded_betas, level_scale)
    inverse = 1.0 / center_weight
    weights = chebyshev_weights(SWEEPS)
    older = jnp.zeros(source.shape, source.dtype)
    current = weights[0][1] * inverse * source
    for sweep_index in range(1, SWEEPS):
        momentum, step_weight = weights[sweep_index]
        newer = chebyshev_sweep(pad_one(current), older, padded_betas, source, center_weight, inverse, level_scale, momentum, step_weight)
        older = current
        current = newer
    residual = source - apply_operator(pad_one(current), padded_betas, center_weight, level_scale)
    return current, residual


def coarsen_cells(field_values):
    span_x, span_y, span_z = field_values.shape
    grouped = field_values.reshape(span_x // 2, 2, span_y // 2, 2, span_z // 2, 2)
    return jnp.mean(grouped, axis=(1, 3, 5))


def coarsen_faces(face_values, normal_dim):
    if normal_dim == 0:
        even_faces = face_values[0::2]
        span_x, span_y, span_z = even_faces.shape
        return jnp.mean(even_faces.reshape(span_x, span_y // 2, 2, span_z // 2, 2), axis=(2, 4))
    if normal_dim == 1:
        even_faces = face_values[:, 0::2]
        span_x, span_y, span_z = even_faces.shape
        return jnp.mean(even_faces.reshape(span_x // 2, 2, span_y, span_z // 2, 2), axis=(1, 4))
    even_faces = face_values[:, :, 0::2]
    span_x, span_y, span_z = even_faces.shape
    return jnp.mean(even_faces.reshape(span_x // 2, 2, span_y // 2, 2, span_z), axis=(1, 3))


def reference(source_term, alpha_cell, beta_x, beta_y, beta_z):
    source = source_term
    alpha_values = alpha_cell
    face_betas = (beta_x, beta_y, beta_z)
    iterates = []
    for level_index in range(LEVELS):
        level_scale = 0.25 ** level_index
        iterate, residual = smooth_level(source, alpha_values, face_betas, level_scale)
        iterates.append(iterate)
        source = coarsen_cells(residual)
        if level_index + 1 < LEVELS:
            alpha_values = coarsen_cells(alpha_values)
            face_betas = (coarsen_faces(face_betas[0], 0), coarsen_faces(face_betas[1], 1), coarsen_faces(face_betas[2], 2))
    return (iterates[0], iterates[1], iterates[2], iterates[3], source)
```

```python
import itertools

import jax
import jax.numpy as jnp
from jax import lax
from jax.experimental import pallas as pl
from jax.experimental.pallas import tpu as pltpu
from jax.sharding import PartitionSpec as P

MESH = pl.DeviceIdType.MESH
AXES = ("gx", "gy", "gz")
SIZES = (8, 8, 4)
SWEEPS = 4
F32 = jnp.float32

SIX = ((1, 0, 0), (-1, 0, 0), (0, 1, 0), (0, -1, 0), (0, 0, 1), (0, 0, -1))
BOX = tuple(d for d in itertools.product((-1, 0, 1), repeat=3) if d != (0, 0, 0))
COLUMNS = tuple(
    d for d in itertools.product((-1, 0, 1), (-1, 0, 1), range(4)) if d != (0, 0, 0)
)
PLANE = tuple(d for d in itertools.product(range(8), range(8), (0,)) if d != (0, 0, 0))

FIELDS = (
    ("a", "pair", "pair", "pair"),
    ("bx", "even", "pair", "pair"),
    ("by", "pair", "even", "pair"),
    ("bz", "pair", "pair", "even"),
    ("hx", "odd", "pair", "pair"),
    ("hy", "pair", "odd", "pair"),
    ("hz", "pair", "pair", "odd"),
)


def chebyshev_weights(count):
    middle, spread = 1.125, 0.875
    sharpness = middle / spread
    weights = [(0.0, 1.0 / middle)]
    rho_prev = 1.0 / sharpness
    for _ in range(1, count):
        rho_next = 1.0 / (2.0 * sharpness - rho_prev)
        weights.append((rho_next * rho_prev, 2.0 * rho_next / spread))
        rho_prev = rho_next
    return weights


WEIGHTS = chebyshev_weights(SWEEPS)


def neighbour(d):
    return tuple(
        lax.rem(lax.axis_index(a) + ((s + n) % n), n) for a, s, n in zip(AXES, d, SIZES)
    )


def iota(shape, dim):
    return lax.broadcasted_iota(jnp.int32, shape, dim)


def roll(value, shift, axis):
    n = value.shape[axis]
    if isinstance(shift, int):
        shift %= n
        if shift == 0:
            return value
    return pltpu.roll(value, shift, axis)


def picker(mode, first, count, out, scale):
    row = iota((128, 128), 0) - first
    col = iota((128, 128), 1) - out
    hit = (row >> 1) == col
    hit = hit & (col >= 0) & (col < count)
    if mode != "pair":
        hit = hit & ((row & 1) == (0 if mode == "even" else 1))
    return jnp.where(hit, scale, 0.0).astype(F32)


def dot(value, matrix):
    return jnp.dot(
        value, matrix, precision=lax.Precision.HIGHEST, preferred_element_type=F32
    )


def x_pick(value, mode):
    n = value.shape[0]
    grouped = value.reshape((n // 2, 2) + value.shape[1:])
    if mode == "pair":
        return grouped[:, 0] + grouped[:, 1]
    return grouped[:, 0 if mode == "even" else 1]


def y_pick(tmp, value, mode):
    rows = value.shape[0]
    tmp[0:rows, :] = value
    if mode == "pair":
        return tmp[pl.ds(0, rows // 2, stride=2), :] + tmp[pl.ds(1, rows // 2, stride=2), :]
    return tmp[pl.ds(0 if mode == "even" else 1, rows // 2, stride=2), :]


def kernel(
    src_h, a_h, bx_h, by_h, bz_h,
    o0_h, o1, o2, o3, o4,
    src, a0, bx, by, bz, hy, hz, diag, inv_s, gain, v,
    send_fx, send_fy, send_fz, next_x, next_y, next_z,
    recv_y, recv_z, send_y, send_z,
    tmp, fold,
    s1c, p1c, s1s, p1s, r1c, q1c, r1s, q1s, k1, u1,
    s2c, s2s, r2c, r2s, k2, u2,
    s3z, r3z, s3c, s3s, r3y, r3c, r3s, k3, u3, x3,
    in_sem, out_sem, send_sem, recv_sem,
):
    gx, gy, gz = (lax.axis_index(a) for a in AXES)
    used = [0]

    def push(source, target, d):
        k = used[0]
        used[0] += 1
        copy = pltpu.make_async_remote_copy(
            src_ref=source,
            dst_ref=target,
            send_sem=send_sem.at[k],
            recv_sem=recv_sem.at[k],
            device_id=neighbour(d),
            device_id_type=MESH,
        )
        copy.start()
        return copy

    def received(copies):
        for copy in copies:
            copy.wait_recv()

    def sent(copies):
        for copy in copies:
            copy.wait_send()

    barrier = pltpu.get_barrier_semaphore()
    for d in SIX:
        pl.semaphore_signal(barrier, inc=1, device_id=neighbour(d), device_id_type=MESH)

    loads = []
    for k, (h, m) in enumerate(
        ((bx_h, bx.at[0:16]), (by_h, by), (bz_h, bz), (a_h, a0), (src_h, src))
    ):
        copy = pltpu.make_async_copy(h, m, in_sem.at[k])
        copy.start()
        loads.append(copy)
    for copy in loads:
        copy.wait()

    lane = iota((8, 128), 1)
    sub = iota((8, 128), 0)
    lane32 = iota((32, 128), 1)
    inner_x = jnp.where(gx > 0, 1.0, 0.0).astype(F32)
    inner_y = jnp.where(gy > 0, 1.0, 0.0).astype(F32)
    inner_z = jnp.where(gz > 0, 1.0, 0.0).astype(F32)

    def pack_ends(packed, value, x):
        for j in range(4):
            at = 32 * j + 2 * x
            moved = roll(value[8 * j : 8 * j + 8, :], at + 1, 1)
            packed = moved if packed is None else jnp.where((lane >> 1) == (at >> 1), moved, packed)
        return packed

    def unpack_ends(ends, x):
        return jnp.concatenate([roll(ends, -(32 * j + 2 * x + 1), 1) for j in range(4)], axis=0)

    send_fx[...] = bx[0] * inner_x
    packed = None
    for x in range(16):
        send_fy[x : x + 1, :] = by[x, 0:1, :] * inner_y
        packed = pack_ends(packed, bz[x], x)
    send_fz[...] = packed * inner_z

    SHAPES = {1: (16, 32), 2: (8, 16), 3: (4, 8)}
    LANES = {1: (0, 64, 64), 2: (64, 32, 0), 3: (0, 16, 0)}
    OWN = {1: {}, 2: {}, 3: {}}

    def coarsen(level, names, fine):
        first, count, out = LANES[level]
        n, m = SHAPES[level]
        matrices = {}
        for k, (name, xm, ym, zm) in enumerate(FIELDS):
            if name not in names:
                continue
            if zm not in matrices:
                matrices[zm] = picker(zm, first, count, out, 1.0)
            value = x_pick(fine(name), xm).reshape(n // 2 * m, 128)
            value = dot(y_pick(tmp, value, ym), matrices[zm])
            OWN[level][k] = value * (0.125 if name == "a" else 0.25)

    INDEX = {f[0]: k for k, f in enumerate(FIELDS)}

    def own(level):
        n, m = SHAPES[level + 1] if level < 3 else (2, 4)
        return lambda name: OWN[level][INDEX[name]].reshape(n, m, 128)

    fine = {"a": a0, "by": by, "bz": bz, "hy": hy, "hz": hz}

    def level_zero(name):
        if name == "bx":
            return bx[0:16]
        if name == "hx":
            return bx[1:17]
        return fine[name][...]

    low = ("a", "bx", "by", "bz")
    high = ("hx", "hy", "hz")
    coarsen(1, low, level_zero)
    coarsen(2, low, own(1))
    coarsen(3, low, own(2))

    pl.semaphore_wait(barrier, 6)

    faces = [
        push(send_fx, next_x, (-1, 0, 0)),
        push(send_fy, next_y, (0, -1, 0)),
        push(send_fz, next_z, (0, 0, -1)),
    ]

    def swap_lanes(from_low, from_high):
        odd = (lane & 1) == 1
        return jnp.where(odd, roll(from_low, 1, 1), roll(from_high, -1, 1))

    def exchange(t):
        for x in range(16):
            send_y[t, 0, x : x + 1, :] = v[t, 1 + x, 8:9, :]
            send_y[t, 1, x : x + 1, :] = v[t, 1 + x, 39:40, :]
        return [
            push(v.at[t, 1, 8:40], v.at[t, 17, 8:40], (-1, 0, 0)),
            push(v.at[t, 16, 8:40], v.at[t, 0, 8:40], (1, 0, 0)),
            push(send_y.at[t, 0], recv_y.at[t, 1], (0, -1, 0)),
            push(send_y.at[t, 1], recv_y.at[t, 0], (0, 1, 0)),
            push(send_z.at[t], recv_z.at[t, 1], (0, 0, -1)),
            push(send_z.at[t], recv_z.at[t, 0], (0, 0, 1)),
        ]

    def land(t):
        for x in range(16):
            v[t, 1 + x, 7:8, :] = recv_y[t, 0, x : x + 1, :]
            v[t, 1 + x, 40:41, :] = recv_y[t, 1, x : x + 1, :]
        return swap_lanes(recv_z[t, 0], recv_z[t, 1])

    def around(t, x, ends):
        c = v[t, 1 + x, 8:40, :]
        halo = unpack_ends(ends, x)
        below = jnp.where(lane32 == 0, halo, roll(c, 1, 1))
        above = jnp.where(lane32 == 127, halo, roll(c, -1, 1))
        total = bx[x] * v[t, x, 8:40, :] + bx[x + 1] * v[t, x + 2, 8:40, :]
        total = total + (by[x] * v[t, 1 + x, 7:39, :] + hy[x] * v[t, 1 + x, 9:41, :])
        return c, total + (bz[x] * below + hz[x] * above)

    received(faces)
    bx[16] = next_x[...]
    ends = roll(next_z[...], -1, 1)
    packed = None
    row32 = iota((32, 128), 0)
    for x in range(16):
        b = by[x]
        up = jnp.where(row32 == 31, jnp.broadcast_to(next_y[x : x + 1, :], (32, 128)), roll(b, -1, 0))
        hy[x] = up
        total = (bx[x] + bx[x + 1]) + (b + up)
        b = bz[x]
        halo = jnp.concatenate([roll(ends, -(32 * j + 2 * x + 1), 1) for j in range(4)], axis=0)
        up = jnp.where(lane32 == 127, halo, roll(b, -1, 1))
        hz[x] = up
        total = a0[x] + (total + (b + up))
        diag[x] = total
        inverse = 1.0 / total
        inv_s[x] = inverse
        g = inverse * src[x]
        gain[x] = g
        g = g * WEIGHTS[0][1]
        v[0, 1 + x, 8:40, :] = g
        packed = pack_ends(packed, g, x)
    send_z[0] = packed
    rounds = [exchange(0)]

    coarsen(1, high, level_zero)
    coarsen(2, high, own(1))
    coarsen(3, high, own(2))
    bx[0] = bx[0] * inner_x
    for x in range(16):
        by[x, 0:1, :] = by[x, 0:1, :] * inner_y
        bz[x] = jnp.where(lane32 == 0, bz[x] * inner_z, bz[x])

    def own_coefficients(level):
        scale = 0.25**level
        get = OWN[level]
        a, lx, ly, lz, ux, uy, uz = (get[k] for k in range(7))
        d = a + scale * ((lx + ux) + (ly + uy) + (lz + uz))
        rows = d.shape[0]
        row = iota((rows, 128), 0)
        m = SHAPES[level][1] // 2
        first = LANES[level][2]
        lx = jnp.where(row < m, lx * inner_x, lx)
        ly = jnp.where((row & (m - 1)) == 0, ly * inner_y, ly)
        lz = jnp.where(iota((rows, 128), 1) == first, lz * inner_z, lz)
        return d, lx, ly, lz

    def pack_one(value):
        lane16 = iota((16, 128), 1) >> 2
        packed = None
        for x in range(8):
            moved = roll(value[16 * x : 16 * x + 16, :], 4 * x + 4, 1)
            if packed is None:
                packed = moved
            else:
                packed = jnp.where((lane16 == x) | (lane16 == x + 17), moved, packed)
        return packed

    def send_one(s, p, r, q):
        copies = []
        for d in BOX:
            dx, dy, dz = d
            xs = {0: pl.ds(0, 8), 1: pl.ds(4, 4), -1: pl.ds(0, 4)}[dx]
            xd = {0: pl.ds(4, 8), 1: pl.ds(0, 4), -1: pl.ds(12, 4)}[dx]
            ys = {0: pl.ds(0, 16), 1: pl.ds(8, 8), -1: pl.ds(0, 8)}[dy]
            yd = {0: pl.ds(0, 16), 1: pl.ds(24, 8), -1: pl.ds(16, 8)}[dy]
            if dz == 0:
                copies.append(push(s.at[:, xs, ys], r.at[:, xd, yd], d))
            else:
                copies.append(push(p.at[:, ys], q.at[:, 0 if dz == 1 else 1, 1 - dx, yd], d))
        return copies

    def ring_rows(value):
        halo = jnp.where(sub < 4, value[16:24, :], value[24:32, :])
        return jnp.concatenate([value[0:16, :], halo], axis=0)

    def assemble_one(r, q, f, out):
        lane24 = iota((24, 128), 1)
        for b, (start, rows) in enumerate(((0, range(4, 8)), (4, range(8)), (12, range(4)))):
            m = ring_rows(jnp.where(lane32 < 64, q[f, 0, b], q[f, 1, b]))
            for n, xl in enumerate(rows):
                c = ring_rows(r[f, start + n])
                out[start + n] = jnp.where(lane24 >= 64, c, roll(m, 60 - 4 * xl, 1))

    fields = own_coefficients(1)
    for f, value in enumerate(fields):
        value3 = value.reshape(8, 16, 128)
        s1c[f] = value3
        r1c[f, 4:12, 0:16, :] = value3
        p1c[f] = pack_one(value)

    def pack_two(value):
        packed = value[0:8, :]
        for x in range(1, 4):
            packed = packed + roll(value[8 * x : 8 * x + 8, :], 32 * x, 1)
        return packed

    def send_two(s, r):
        return [push(s, r.at[1 - d[0], 1 - d[1], gz], d) for d in COLUMNS]

    def assemble_two(get, out):
        for b in range(3):
            for t in range(2):
                tiles = []
                for z in range(4):
                    if t == 0:
                        tiles.append(get(b, 1, z))
                    else:
                        tiles.append(jnp.where(sub < 4, get(b, 2, z), get(b, 0, z)))
                for x in range(4):
                    value = roll(tiles[0], -32 * x, 1)
                    for z in range(1, 4):
                        value = jnp.where((lane >> 5) == z, roll(tiles[z], 32 * (z - x), 1), value)
                    out[4 * b + x, 8 * t : 8 * t + 8, :] = value

    def sweep(t):
        momentum, step = WEIGHTS[t + 1]
        ends = land(t)
        packed = None
        for x in range(16):
            c, total = around(t, x, ends)
            new = (1.0 + momentum - step) * c + step * (gain[x] + inv_s[x] * total)
            if t > 0:
                new = new - momentum * v[t - 1, 1 + x, 8:40, :]
            v[t + 1, 1 + x, 8:40, :] = new
            packed = pack_ends(packed, new, x)
        send_z[t + 1] = packed
        rounds.append(exchange(t + 1))

    sent(faces)
    received(rounds[0])
    sweep(0)

    for f, value in enumerate(own_coefficients(2)):
        s2c[f] = pack_two(value)
    r2c[1, 1, gz] = s2c[...]
    for f, value in enumerate(own_coefficients(3)):
        halves = jnp.where(sub < 4, value, roll(value, 64, 1))
        halves = halves + roll(halves, 4, 0)
        s3z[f] = roll(halves, 16 * gz, 1)[0:4, :]
    r3z[gz] = s3z[...]
    three_columns = [push(s3z, r3z.at[gz], (0, 0, d)) for d in (1, 2, 3)]

    sent(rounds[0])
    received(rounds[1])
    sweep(1)

    one_coefficients = send_one(s1c, p1c, r1c, q1c)
    received(three_columns)
    s3c[...] = (r3z[0] + r3z[1]) + (r3z[2] + r3z[3])
    r3y[gy] = s3c[...]
    sent(three_columns)

    def prepare(k, planes, scale):
        for x in range(planes):
            d = k[0, x]
            inverse = 1.0 / jnp.where(d > 0, d, 1.0)
            k[4, x] = inverse
            k[5, x] = scale * inverse
            k[6, x] = roll(k[2, x], -1, 0)
            k[7, x] = roll(k[3, x], -1, 1)

    sent(rounds[1])
    received(rounds[2])
    sweep(2)

    result = pltpu.make_async_copy(v.at[3, 1:17, 8:40], o0_h, out_sem)
    result.start()

    two_coefficients = send_two(s2c, r2c)
    three_rows = [push(s3c, r3y.at[gy], (0, d, 0)) for d in range(1, 8)]
    received(one_coefficients)
    for f in range(4):
        assemble_one(r1c, q1c, f, k1.at[f])
    prepare(k1, 16, 0.25)
    sent(one_coefficients)
    sent(rounds[2])
    received(rounds[3])

    ends = land(3)
    for x in range(0, 16, 2):
        pair = None
        for y in (x, x + 1):
            c, total = around(3, y, ends)
            r = (src[y] - diag[y] * c) + total
            pair = r if pair is None else pair + r
        fold[16 * x : 16 * x + 32, :] = pair
    value = fold[pl.ds(0, 128, stride=2), :] + fold[pl.ds(1, 128, stride=2), :]
    value = dot(value, picker("pair", 0, 64, 64, 0.125))
    s1s[0] = value.reshape(8, 16, 128)
    r1s[0, 4:12, 0:16, :] = s1s[0]
    p1s[0] = pack_one(value)
    one_source = send_one(s1s, p1s, r1s, q1s)

    received(three_rows)
    r3c[gx] = r3y[...]
    three_coefficients = [push(r3y, r3c.at[gx], (d, 0, 0)) for d in range(1, 8)]
    received(two_coefficients)
    for f in range(4):
        assemble_two(lambda b, y, z, f=f: r2c[b, y, z, f], k2.at[f])
    prepare(k2, 12, 0.25**2)
    sent(two_coefficients)
    sent(three_rows)
    sent(rounds[3])
    received(one_source)

    def wide_around(k, c, lower, upper, x):
        total = k[1, x] * lower + k[1, x + 1] * upper
        total = total + (k[2, x] * roll(c, 1, 0) + k[6, x] * roll(c, -1, 0))
        return total + (k[3, x] * roll(c, 1, 1) + k[7, x] * roll(c, -1, 1))

    def wide_level(k, u, planes):
        for x in range(planes):
            g = k[4, x] * k[8, x]
            k[9, x] = g
            u[0, x] = WEIGHTS[0][1] * g
        for t in range(1, SWEEPS):
            momentum, step = WEIGHTS[t]
            for x in range(t, planes - t):
                c = u[t - 1, x]
                total = wide_around(k, c, u[t - 1, x - 1], u[t - 1, x + 1], x)
                new = (1.0 + momentum - step) * c + step * (k[9, x] + k[5, x] * total)
                if t > 1:
                    new = new - momentum * u[t - 2, x]
                u[t, x] = new

    def wide_residual(k, u, x, scale):
        c = u[3, x]
        total = wide_around(k, c, u[3, x - 1], u[3, x + 1], x)
        return (k[8, x] - k[0, x] * c) + scale * total

    assemble_one(r1s, q1s, 0, k1.at[8])
    wide_level(k1, u1, 16)
    lane16 = iota((16, 128), 1)
    for x in range(4):
        r = wide_residual(k1, u1, 4 + 2 * x, 0.25) + wide_residual(k1, u1, 5 + 2 * x, 0.25)
        fold[16 * x : 16 * x + 16, :] = jnp.where(lane16 >= 64, r[0:16, :], 0.0)
    value = fold[pl.ds(0, 32, stride=2), :] + fold[pl.ds(1, 32, stride=2), :]
    value = dot(value, picker("pair", 64, 32, 0, 0.125))
    s2s[...] = pack_two(value)
    r2s[1, 1, gz] = s2s[...]
    two_source = send_two(s2s, r2s)
    for x in range(8):
        o1[x] = roll(u1[3, 4 + x, 0:16, :], 64, 1)[:, 0:64]
    received(three_coefficients)
    for y in range(8):
        for f in range(4):
            k3[f, :, 4 * y : 4 * y + 4, :] = r3c[:, y, f]
    lane8 = iota((32, 128), 1)
    for x in range(8):
        inverse = 1.0 / k3[0, x]
        k3[4, x] = inverse
        k3[5, x] = 0.25**3 * inverse
        k3[6, x] = roll(k3[2, x], -1, 0)
        k3[7, x] = roll(k3[3, x], -1, 1)
        here, after = roll(k3[1, x], 64, 1), roll(k3[1, (x + 1) % 8], 64, 1)
        k3[10, x] = jnp.where(lane8 < 64, here, after)
    sent(one_source)
    sent(three_coefficients)
    received(two_source)

    assemble_two(lambda b, y, z: r2s[b, y, z], k2.at[8])
    wide_level(k2, u2, 12)
    for x in range(2):
        r = wide_residual(k2, u2, 4 + 2 * x, 0.25**2) + wide_residual(k2, u2, 5 + 2 * x, 0.25**2)
        fold[8 * x : 8 * x + 8, :] = r[0:8, :]
    value = fold[pl.ds(0, 8, stride=2), :] + fold[pl.ds(1, 8, stride=2), :]
    value = dot(value, picker("pair", 0, 64, 0, 0.125))
    halves = jnp.where(sub < 4, value, roll(value, 64, 1))
    s3s[...] = (halves + roll(halves, 4, 0))[0:4, :]
    r3s[gx, gy] = s3s[...]
    three_source = [push(s3s, r3s.at[gx, gy], d) for d in PLANE]
    for x in range(4):
        o2[x] = roll(u2[3, 4 + x, 0:8, :], 128 - 32 * gz, 1)[:, 0:32]
    sent(two_source)
    received(three_source)

    for y in range(8):
        k3[8, :, 4 * y : 4 * y + 4, :] = r3s[:, y]

    def whole_around(t, x):
        c = u3[t, x]
        turned = roll(c, 64, 1)
        lower = jnp.where(lane8 < 64, roll(u3[t, (x + 7) % 8], 64, 1), turned)
        upper = jnp.where(lane8 < 64, turned, roll(u3[t, (x + 1) % 8], 64, 1))
        total = k3[1, x] * lower + k3[10, x] * upper
        total = total + (k3[2, x] * roll(c, 1, 0) + k3[6, x] * roll(c, -1, 0))
        return c, total + (k3[3, x] * roll(c, 1, 1) + k3[7, x] * roll(c, -1, 1))

    for x in range(8):
        g = k3[4, x] * k3[8, x]
        k3[9, x] = g
        u3[0, x] = WEIGHTS[0][1] * g
    for t in range(1, SWEEPS):
        momentum, step = WEIGHTS[t]
        for x in range(8):
            c, total = whole_around(t - 1, x)
            new = (1.0 + momentum - step) * c + step * (k3[9, x] + k3[5, x] * total)
            if t > 1:
                new = new - momentum * u3[t - 2, x]
            u3[t, x] = new
    for x in range(8):
        c, total = whole_around(3, x)
        r = (k3[8, x] - k3[0, x] * c) + 0.25**3 * total
        fold[32 * x : 32 * x + 32, :] = r + roll(r, 64, 1)
        for y in range(8):
            x3[x, y, 0:4, :] = c[4 * y : 4 * y + 4, :]
    value = fold[pl.ds(0, 128, stride=2), :] + fold[pl.ds(1, 128, stride=2), :]
    value = dot(value, picker("pair", 0, 32, 0, 0.125))
    o4[...] = value.reshape(8, 16, 128)[:, :, 0:32]
    mine = x3[gx, gy]
    for half in range(2):
        o3[half] = roll(mine, (128 - 64 * half) - 16 * gz, 1)[0:4, 0:16]
    sent(three_source)
    result.wait()


def body(*args):
    vm = lambda *shape: pltpu.VMEM(shape, F32)
    scratch = [
        vm(16, 32, 128), vm(16, 32, 128), vm(17, 32, 128), vm(16, 32, 128), vm(16, 32, 128),
        vm(16, 32, 128), vm(16, 32, 128), vm(16, 32, 128), vm(16, 32, 128), vm(16, 32, 128),
        vm(4, 18, 48, 128),
        vm(32, 128), vm(16, 128), vm(8, 128), vm(32, 128), vm(16, 128), vm(8, 128),
        vm(4, 2, 16, 128), vm(4, 2, 8, 128), vm(4, 2, 16, 128), vm(4, 8, 128),
        vm(256, 128), vm(256, 128),
        vm(4, 8, 16, 128), vm(4, 16, 128), vm(1, 8, 16, 128), vm(1, 16, 128),
        vm(4, 16, 32, 128), vm(4, 2, 3, 32, 128), vm(1, 16, 32, 128), vm(1, 2, 3, 32, 128),
        vm(10, 16, 24, 128), vm(4, 16, 24, 128),
        vm(4, 8, 128), vm(8, 128), vm(3, 3, 4, 4, 8, 128), vm(3, 3, 4, 8, 128),
        vm(10, 12, 16, 128), vm(4, 12, 16, 128),
        vm(4, 4, 128), vm(4, 4, 4, 128), vm(4, 4, 128), vm(4, 128),
        vm(8, 4, 4, 128), vm(8, 8, 4, 4, 128), vm(8, 8, 4, 128), vm(11, 8, 32, 128), vm(4, 8, 32, 128),
        vm(8, 8, 8, 128),
        pltpu.SemaphoreType.DMA((5,)), pltpu.SemaphoreType.DMA,
        pltpu.SemaphoreType.DMA((288,)), pltpu.SemaphoreType.DMA((288,)),
    ]
    out = lambda *shape: jax.ShapeDtypeStruct(shape, F32)
    return pl.pallas_call(
        kernel,
        out_shape=(out(16, 32, 128), out(8, 16, 64), out(4, 8, 32), out(2, 4, 16), out(8, 16, 32)),
        in_specs=[pl.BlockSpec(memory_space=pl.ANY)] * 5,
        out_specs=[pl.BlockSpec(memory_space=pl.ANY)] + [pl.BlockSpec(memory_space=pltpu.VMEM)] * 4,
        scratch_shapes=scratch,
        compiler_params=pltpu.CompilerParams(
            collective_id=0, has_side_effects=True, vmem_limit_bytes=48 * 2**20
        ),
    )(*args)


def solution(mesh):
    spec = P(*AXES)
    return jax.shard_map(
        body,
        mesh=mesh,
        in_specs=(spec,) * 5,
        out_specs=(spec, spec, spec, spec, P()),
        check_vma=False,
    )
```

```python
import itertools

import jax
import jax.numpy as jnp
from jax import lax
from jax.experimental import pallas as pl
from jax.experimental.pallas import tpu as pltpu
from jax.sharding import PartitionSpec as P

MESH = pl.DeviceIdType.MESH
AXES = ("gx", "gy", "gz")
SIZES = (8, 8, 4)
SWEEPS = 4
F32 = jnp.float32


def distance(d):
    return sum(min(s % n, -s % n) for s, n in zip(d, SIZES))


def farthest_first(xs, ys, zs):
    directions = [d for d in itertools.product(xs, ys, zs) if d != (0, 0, 0)]
    return tuple(sorted(directions, key=lambda d: -distance(d)))


BOX = farthest_first((-1, 0, 1), (-1, 0, 1), (-1, 0, 1))
COLUMNS = farthest_first((-1, 0, 1), (-1, 0, 1), (0, 1, 2, 3))
PLANE = farthest_first(range(8), range(8), (0,))
SIX = tuple(d for d in BOX if distance(d) == 1)

FIELDS = (
    ("a", "pair", "pair", "pair"),
    ("bx", "even", "pair", "pair"),
    ("by", "pair", "even", "pair"),
    ("bz", "pair", "pair", "even"),
    ("hx", "odd", "pair", "pair"),
    ("hy", "pair", "odd", "pair"),
    ("hz", "pair", "pair", "odd"),
)


def chebyshev_weights(count):
    middle, spread = 1.125, 0.875
    sharpness = middle / spread
    weights = [(0.0, 1.0 / middle)]
    rho_prev = 1.0 / sharpness
    for _ in range(1, count):
        rho_next = 1.0 / (2.0 * sharpness - rho_prev)
        weights.append((rho_next * rho_prev, 2.0 * rho_next / spread))
        rho_prev = rho_next
    return weights


WEIGHTS = chebyshev_weights(SWEEPS)


def neighbour(d):
    return tuple(
        lax.rem(lax.axis_index(a) + ((s + n) % n), n) for a, s, n in zip(AXES, d, SIZES)
    )


def iota(shape, dim):
    return lax.broadcasted_iota(jnp.int32, shape, dim)


def roll(value, shift, axis):
    n = value.shape[axis]
    if isinstance(shift, int):
        shift %= n
        if shift == 0:
            return value
    return pltpu.roll(value, shift, axis)


def picker(mode, first, count, out, scale):
    row = iota((128, 128), 0) - first
    col = iota((128, 128), 1) - out
    hit = (row >> 1) == col
    hit = hit & (col >= 0) & (col < count)
    if mode != "pair":
        hit = hit & ((row & 1) == (0 if mode == "even" else 1))
    return jnp.where(hit, scale, 0.0).astype(F32)


def dot(value, matrix):
    return jnp.dot(
        value, matrix, precision=lax.Precision.HIGHEST, preferred_element_type=F32
    )


def x_pick(value, mode):
    n = value.shape[0]
    grouped = value.reshape((n // 2, 2) + value.shape[1:])
    if mode == "pair":
        return grouped[:, 0] + grouped[:, 1]
    return grouped[:, 0 if mode == "even" else 1]


def y_pick(tmp, value, mode):
    rows = value.shape[0]
    tmp[0:rows, :] = value
    if mode == "pair":
        return tmp[pl.ds(0, rows // 2, stride=2), :] + tmp[pl.ds(1, rows // 2, stride=2), :]
    return tmp[pl.ds(0 if mode == "even" else 1, rows // 2, stride=2), :]


def kernel(
    src_h, a_h, bx_h, by_h, bz_h,
    o0_h, o1, o2, o3, o4,
    src, a0, bx, by, bz, hy, hz, diag, inv_s, gain, v,
    send_fx, send_fy, send_fz, next_x, next_y, next_z,
    recv_y, recv_z, send_y, send_z,
    tmp, fold,
    s1c, p1c, s1s, p1s, r1c, q1c, r1s, q1s, k1, u1,
    s2c, s2s, r2c, r2s, k2, u2,
    r3, s3s, r3s, k3, u3, x3,
    in_sem, out_sem, send_sem, recv_sem,
):
    gx, gy, gz = (lax.axis_index(a) for a in AXES)
    used = [0]

    def push(source, target, d, device=None):
        k = used[0]
        used[0] += 1
        copy = pltpu.make_async_remote_copy(
            src_ref=source,
            dst_ref=target,
            send_sem=send_sem.at[k],
            recv_sem=recv_sem.at[k],
            device_id=neighbour(d) if device is None else device,
            device_id_type=MESH,
        )
        copy.start()
        return copy

    def received(copies):
        for copy in copies:
            copy.wait_recv()

    def sent(copies):
        for copy in copies:
            copy.wait_send()

    barrier = pltpu.get_barrier_semaphore()
    for d in SIX:
        pl.semaphore_signal(barrier, inc=1, device_id=neighbour(d), device_id_type=MESH)

    loads = []
    for k, (h, m) in enumerate(
        ((bx_h, bx.at[0:16]), (by_h, by), (bz_h, bz), (a_h, a0), (src_h, src))
    ):
        copy = pltpu.make_async_copy(h, m, in_sem.at[k])
        copy.start()
        loads.append(copy)
    for copy in loads:
        copy.wait()

    lane = iota((8, 128), 1)
    sub = iota((8, 128), 0)
    lane32 = iota((32, 128), 1)
    inner_x = jnp.where(gx > 0, 1.0, 0.0).astype(F32)
    inner_y = jnp.where(gy > 0, 1.0, 0.0).astype(F32)
    inner_z = jnp.where(gz > 0, 1.0, 0.0).astype(F32)

    def pack_ends(packed, value, x):
        for j in range(4):
            at = 32 * j + 2 * x
            moved = roll(value[8 * j : 8 * j + 8, :], at + 1, 1)
            packed = moved if packed is None else jnp.where((lane >> 1) == (at >> 1), moved, packed)
        return packed

    def unpack_ends(ends, x):
        return jnp.concatenate([roll(ends, -(32 * j + 2 * x + 1), 1) for j in range(4)], axis=0)

    send_fx[...] = bx[0] * inner_x
    packed = None
    for x in range(16):
        send_fy[x : x + 1, :] = by[x, 0:1, :] * inner_y
        packed = pack_ends(packed, bz[x], x)
    send_fz[...] = packed * inner_z

    SHAPES = {1: (16, 32), 2: (8, 16), 3: (4, 8)}
    LANES = {1: (0, 64, 64), 2: (64, 32, 0), 3: (0, 16, 0)}
    OWN = {1: {}, 2: {}, 3: {}}

    def coarsen(level, names, fine):
        first, count, out = LANES[level]
        n, m = SHAPES[level]
        matrices = {}
        for k, (name, xm, ym, zm) in enumerate(FIELDS):
            if name not in names:
                continue
            if zm not in matrices:
                matrices[zm] = picker(zm, first, count, out, 1.0)
            value = x_pick(fine(name), xm).reshape(n // 2 * m, 128)
            value = dot(y_pick(tmp, value, ym), matrices[zm])
            OWN[level][k] = value * (0.125 if name == "a" else 0.25)

    INDEX = {f[0]: k for k, f in enumerate(FIELDS)}

    def own(level):
        n, m = SHAPES[level + 1] if level < 3 else (2, 4)
        return lambda name: OWN[level][INDEX[name]].reshape(n, m, 128)

    fine = {"a": a0, "by": by, "bz": bz, "hy": hy, "hz": hz}

    def level_zero(name):
        if name == "bx":
            return bx[0:16]
        if name == "hx":
            return bx[1:17]
        return fine[name][...]

    low = ("a", "bx", "by", "bz")
    high = ("hx", "hy", "hz")

    pl.semaphore_wait(barrier, 6)

    faces = [
        push(send_fx, next_x, (-1, 0, 0)),
        push(send_fy, next_y, (0, -1, 0)),
        push(send_fz, next_z, (0, 0, -1)),
    ]

    def swap_lanes(from_low, from_high):
        odd = (lane & 1) == 1
        return jnp.where(odd, roll(from_low, 1, 1), roll(from_high, -1, 1))

    ORDER = (0, 15) + tuple(range(1, 15))

    def exchange_x(t):
        return [
            push(v.at[t, 1, 8:40], v.at[t, 17, 8:40], (-1, 0, 0)),
            push(v.at[t, 16, 8:40], v.at[t, 0, 8:40], (1, 0, 0)),
        ]

    def exchange_yz(t):
        for x in range(16):
            send_y[t, 0, x : x + 1, :] = v[t, 1 + x, 8:9, :]
            send_y[t, 1, x : x + 1, :] = v[t, 1 + x, 39:40, :]
        return [
            push(send_z.at[t], recv_z.at[t, 1], (0, 0, -1)),
            push(send_z.at[t], recv_z.at[t, 0], (0, 0, 1)),
            push(send_y.at[t, 0], recv_y.at[t, 1], (0, -1, 0)),
            push(send_y.at[t, 1], recv_y.at[t, 0], (0, 1, 0)),
        ]

    def land(t):
        for x in range(16):
            v[t, 1 + x, 7:8, :] = recv_y[t, 0, x : x + 1, :]
            v[t, 1 + x, 40:41, :] = recv_y[t, 1, x : x + 1, :]
        return swap_lanes(recv_z[t, 0], recv_z[t, 1])

    def around(t, x, ends):
        c = v[t, 1 + x, 8:40, :]
        halo = unpack_ends(ends, x)
        below = jnp.where(lane32 == 0, halo, roll(c, 1, 1))
        above = jnp.where(lane32 == 127, halo, roll(c, -1, 1))
        total = bx[x] * v[t, x, 8:40, :] + bx[x + 1] * v[t, x + 2, 8:40, :]
        total = total + (by[x] * v[t, 1 + x, 7:39, :] + hy[x] * v[t, 1 + x, 9:41, :])
        return c, total + (bz[x] * below + hz[x] * above)

    received(faces)
    bx[16] = next_x[...]
    ends = roll(next_z[...], -1, 1)
    packed = None
    row32 = iota((32, 128), 0)
    for x in ORDER:
        b = by[x]
        up = jnp.where(row32 == 31, jnp.broadcast_to(next_y[x : x + 1, :], (32, 128)), roll(b, -1, 0))
        hy[x] = up
        total = (bx[x] + bx[x + 1]) + (b + up)
        b = bz[x]
        halo = jnp.concatenate([roll(ends, -(32 * j + 2 * x + 1), 1) for j in range(4)], axis=0)
        up = jnp.where(lane32 == 127, halo, roll(b, -1, 1))
        hz[x] = up
        total = a0[x] + (total + (b + up))
        diag[x] = total
        inverse = 1.0 / total
        inv_s[x] = inverse
        g = inverse * src[x]
        gain[x] = g
        g = g * WEIGHTS[0][1]
        v[0, 1 + x, 8:40, :] = g
        packed = pack_ends(packed, g, x)
        if x == 15:
            rounds = [exchange_x(0)]
    send_z[0] = packed
    rounds[0] += exchange_yz(0)

    coarsen(1, low, level_zero)
    coarsen(2, low, own(1))
    coarsen(3, low, own(2))
    coarsen(1, high, level_zero)
    coarsen(2, high, own(1))
    coarsen(3, high, own(2))
    bx[0] = bx[0] * inner_x
    for x in range(16):
        by[x, 0:1, :] = by[x, 0:1, :] * inner_y
        bz[x] = jnp.where(lane32 == 0, bz[x] * inner_z, bz[x])

    def own_coefficients(level):
        scale = 0.25**level
        get = OWN[level]
        a, lx, ly, lz, ux, uy, uz = (get[k] for k in range(7))
        d = a + scale * ((lx + ux) + (ly + uy) + (lz + uz))
        rows = d.shape[0]
        row = iota((rows, 128), 0)
        m = SHAPES[level][1] // 2
        first = LANES[level][2]
        lx = jnp.where(row < m, lx * inner_x, lx)
        ly = jnp.where((row & (m - 1)) == 0, ly * inner_y, ly)
        lz = jnp.where(iota((rows, 128), 1) == first, lz * inner_z, lz)
        return d, lx, ly, lz

    def pack_one(value):
        lane16 = iota((16, 128), 1) >> 2
        packed = None
        for x in range(8):
            moved = roll(value[16 * x : 16 * x + 16, :], 4 * x + 4, 1)
            if packed is None:
                packed = moved
            else:
                packed = jnp.where((lane16 == x) | (lane16 == x + 17), moved, packed)
        return packed

    def send_one(s, p, r, q, reach):
        copies = []
        for d in BOX:
            if distance(d) not in reach:
                continue
            dx, dy, dz = d
            xs = {0: pl.ds(0, 8), 1: pl.ds(4, 4), -1: pl.ds(0, 4)}[dx]
            xd = {0: pl.ds(4, 8), 1: pl.ds(0, 4), -1: pl.ds(12, 4)}[dx]
            ys = {0: pl.ds(0, 16), 1: pl.ds(12, 4), -1: pl.ds(0, 4)}[dy]
            yd = {0: pl.ds(0, 16), 1: pl.ds(20, 4), -1: pl.ds(16, 4)}[dy]
            if dz == 0:
                copies.append(push(s.at[:, xs, ys], r.at[:, xd, yd], d))
            else:
                copies.append(push(p.at[:, ys], q.at[:, 0 if dz == 1 else 1, 1 - dx, yd], d))
        return copies

    lane24 = iota((24, 128), 1)

    def assemble_one(get, q, f, out):
        for b, (start, rows) in enumerate(((0, range(4, 8)), (4, range(8)), (12, range(4)))):
            m = jnp.where(lane24 < 64, q[f, 0, b], q[f, 1, b])
            for n, xl in enumerate(rows):
                out[start + n] = jnp.where(lane24 >= 64, get(start + n), roll(m, 60 - 4 * xl, 1))

    fields = own_coefficients(1)
    for f, value in enumerate(fields):
        p1c[f] = pack_one(value)
    for f in range(2):
        value = (fields[2 * f] + roll(fields[2 * f + 1], 64, 1)).reshape(8, 16, 128)
        s1c[f] = value
        r1c[f, 4:12, 0:16, :] = value
    one_coefficients = send_one(s1c, p1c, r1c, q1c, (1,))

    def pack_two(value):
        packed = value[0:8, :]
        for x in range(1, 4):
            packed = packed + roll(value[8 * x : 8 * x + 8, :], 32 * x, 1)
        return packed

    def send_two(s, r, reach):
        copies = []
        for d in COLUMNS:
            if distance(d) not in reach:
                continue
            target = r.at[1 - d[0], 1 if d[1] else 0, gz]
            if d[1] == 0:
                copies.append(push(s, target, d))
            else:
                half = pl.ds(4, 4) if d[1] == 1 else pl.ds(0, 4)
                copies.append(push(s.at[:, half], target.at[:, half], d))
        return copies

    def assemble_two(get, out):
        for b in range(3):
            for t in range(2):
                tiles = [get(b, t, z) for z in range(4)]
                for x in range(4):
                    value = roll(tiles[0], -32 * x, 1)
                    for z in range(1, 4):
                        value = jnp.where((lane >> 5) == z, roll(tiles[z], 32 * (z - x), 1), value)
                    out[4 * b + x, 8 * t : 8 * t + 8, :] = value

    def sweep(t):
        momentum, step = WEIGHTS[t + 1]
        ends = land(t)
        packed = None
        for x in ORDER:
            c, total = around(t, x, ends)
            new = (1.0 + momentum - step) * c + step * (gain[x] + inv_s[x] * total)
            if t > 0:
                new = new - momentum * v[t - 1, 1 + x, 8:40, :]
            v[t + 1, 1 + x, 8:40, :] = new
            packed = pack_ends(packed, new, x)
            if x == 15:
                rounds.append(exchange_x(t + 1))
        send_z[t + 1] = packed
        rounds[t + 1] += exchange_yz(t + 1)

    sent(faces)
    received(rounds[0])
    sweep(0)

    one_coefficients += send_one(s1c, p1c, r1c, q1c, (2,))
    for f, value in enumerate(own_coefficients(2)):
        s2c[f] = pack_two(value)
    r2c[1, 0, gz] = s2c[...]
    halves_of = lambda value: jnp.where(sub < 4, value, roll(value, 64, 1))
    total = None
    for f, value in enumerate(own_coefficients(3)):
        halves = halves_of(value)
        halves = roll(halves + roll(halves, 4, 0), 16 * f, 1)
        total = halves if total is None else total + halves
    parity, chip = gy % 2, gy // 2
    r3[parity, chip, gz, gx] = total[0:4, :]

    sent(rounds[0])
    received(rounds[1])
    sweep(1)
    one_coefficients += send_one(s1c, p1c, r1c, q1c, (3,))
    two_coefficients = send_two(s2c, r2c, (1, 2, 3))

    def prepare(k, planes, scale):
        for x in range(planes):
            d = k[0, x]
            inverse = 1.0 / jnp.where(d > 0, d, 1.0)
            k[4, x] = inverse
            k[5, x] = scale * inverse
            k[6, x] = roll(k[2, x], -1, 0)
            k[7, x] = roll(k[3, x], -1, 1)

    sent(rounds[1])
    received(rounds[2])
    sweep(2)
    two_coefficients += send_two(s2c, r2c, (4,))
    block = r3.at[parity, chip, gz, gx]
    three_x = [push(block, block, (d, 0, 0)) for d in (4, 3, 5, 2, 6, 1, 7)]

    result = pltpu.make_async_copy(v.at[3, 1:17, 8:40], o0_h, out_sem)
    result.start()

    received(one_coefficients)
    for f in range(4):
        if f % 2 == 0:
            assemble_one(lambda x, f=f: r1c[f // 2, x], q1c, f, k1.at[f])
        else:
            assemble_one(lambda x, f=f: roll(r1c[f // 2, x], 64, 1), q1c, f, k1.at[f])
    prepare(k1, 16, 0.25)
    sent(one_coefficients)
    sent(rounds[2])
    received(rounds[3])

    ends = land(3)
    for x in range(0, 16, 2):
        pair = None
        for y in (x, x + 1):
            c, total = around(3, y, ends)
            r = (src[y] - diag[y] * c) + total
            pair = r if pair is None else pair + r
        fold[16 * x : 16 * x + 32, :] = pair
    value = fold[pl.ds(0, 128, stride=2), :] + fold[pl.ds(1, 128, stride=2), :]
    value = dot(value, picker("pair", 0, 64, 64, 0.125))
    s1s[0] = value.reshape(8, 16, 128)
    r1s[0, 4:12, 0:16, :] = s1s[0]
    p1s[0] = pack_one(value)
    one_source = send_one(s1s, p1s, r1s, q1s, (1, 2, 3))

    received(three_x)
    block = r3.at[parity, chip, gz]
    three_z = [push(block, block, (0, 0, d)) for d in (2, 1, 3)]
    received(two_coefficients)
    for f in range(4):
        assemble_two(lambda b, t, z, f=f: r2c[b, t, z, f], k2.at[f])
    prepare(k2, 12, 0.25**2)
    sent(two_coefficients)
    sent(three_x)
    received(three_z)
    block = r3.at[parity, chip]
    three_y = [push(block, block, (0, d, 0)) for d in (4, 2, 6)]
    sent(rounds[3])
    received(one_source)

    def wide_around(k, c, lower, upper, x):
        total = k[1, x] * lower + k[1, x + 1] * upper
        total = total + (k[2, x] * roll(c, 1, 0) + k[6, x] * roll(c, -1, 0))
        return total + (k[3, x] * roll(c, 1, 1) + k[7, x] * roll(c, -1, 1))

    def wide_level(k, u, planes):
        for x in range(planes):
            g = k[4, x] * k[8, x]
            k[9, x] = g
            u[0, x] = WEIGHTS[0][1] * g
        for t in range(1, SWEEPS):
            momentum, step = WEIGHTS[t]
            for x in range(t, planes - t):
                c = u[t - 1, x]
                total = wide_around(k, c, u[t - 1, x - 1], u[t - 1, x + 1], x)
                new = (1.0 + momentum - step) * c + step * (k[9, x] + k[5, x] * total)
                if t > 1:
                    new = new - momentum * u[t - 2, x]
                u[t, x] = new

    def wide_residual(k, u, x, scale):
        c = u[3, x]
        total = wide_around(k, c, u[3, x - 1], u[3, x + 1], x)
        return (k[8, x] - k[0, x] * c) + scale * total

    assemble_one(lambda x: r1s[0, x], q1s, 0, k1.at[8])
    wide_level(k1, u1, 16)
    lane16 = iota((16, 128), 1)
    for x in range(4):
        r = wide_residual(k1, u1, 4 + 2 * x, 0.25) + wide_residual(k1, u1, 5 + 2 * x, 0.25)
        fold[16 * x : 16 * x + 16, :] = jnp.where(lane16 >= 64, r[0:16, :], 0.0)
    value = fold[pl.ds(0, 32, stride=2), :] + fold[pl.ds(1, 32, stride=2), :]
    value = dot(value, picker("pair", 64, 32, 0, 0.125))
    s2s[0] = pack_two(value)
    r2s[1, 0, gz] = s2s[...]
    two_source = send_two(s2s, r2s, (1, 2, 3, 4))
    sent(three_z)
    received(three_y)
    block = r3.at[parity]
    three_core = [push(block, block, None, (gx, gy + 1 - 2 * parity, gz))]
    for x in range(8):
        o1[x] = roll(u1[3, 4 + x, 0:16, :], 64, 1)[:, 0:64]
    received(three_core)
    group = (lane >> 4) & 3
    for x in range(8):
        for p in range(4):
            tiles = [jnp.concatenate([r3[0, p, z, x], r3[1, p, z, x]], axis=0) for z in range(4)]
            for f in range(4):
                value = roll(tiles[0], -16 * f, 1)
                for z in range(1, 4):
                    value = jnp.where(group == z, roll(tiles[z], 16 * (z - f), 1), value)
                k3[f, x, 8 * p : 8 * p + 8, :] = value
    lane8 = iota((32, 128), 1)
    for x in range(8):
        inverse = 1.0 / k3[0, x]
        k3[4, x] = inverse
        k3[5, x] = 0.25**3 * inverse
        k3[6, x] = roll(k3[2, x], -1, 0)
        k3[7, x] = roll(k3[3, x], -1, 1)
        here, after = roll(k3[1, x], 64, 1), roll(k3[1, (x + 1) % 8], 64, 1)
        k3[10, x] = jnp.where(lane8 < 64, here, after)
    sent(one_source)
    sent(three_y)
    received(two_source)

    assemble_two(lambda b, t, z: r2s[b, t, z, 0], k2.at[8])
    wide_level(k2, u2, 12)
    for x in range(2):
        r = wide_residual(k2, u2, 4 + 2 * x, 0.25**2) + wide_residual(k2, u2, 5 + 2 * x, 0.25**2)
        fold[8 * x : 8 * x + 8, :] = r[0:8, :]
    value = fold[pl.ds(0, 8, stride=2), :] + fold[pl.ds(1, 8, stride=2), :]
    value = dot(value, picker("pair", 0, 64, 0, 0.125))
    halves = halves_of(value)
    s3s[...] = (halves + roll(halves, 4, 0))[0:4, :]
    r3s[gx, gy] = s3s[...]
    three_source = [push(s3s, r3s.at[gx, gy], d) for d in PLANE]
    for x in range(4):
        o2[x] = roll(u2[3, 4 + x, 0:8, :], 128 - 32 * gz, 1)[:, 0:32]
    sent(two_source)
    sent(three_core)
    received(three_source)

    for y in range(8):
        k3[8, :, 4 * y : 4 * y + 4, :] = r3s[:, y]

    def whole_around(t, x):
        c = u3[t, x]
        turned = roll(c, 64, 1)
        lower = jnp.where(lane8 < 64, roll(u3[t, (x + 7) % 8], 64, 1), turned)
        upper = jnp.where(lane8 < 64, turned, roll(u3[t, (x + 1) % 8], 64, 1))
        total = k3[1, x] * lower + k3[10, x] * upper
        total = total + (k3[2, x] * roll(c, 1, 0) + k3[6, x] * roll(c, -1, 0))
        return c, total + (k3[3, x] * roll(c, 1, 1) + k3[7, x] * roll(c, -1, 1))

    for x in range(8):
        g = k3[4, x] * k3[8, x]
        k3[9, x] = g
        u3[0, x] = WEIGHTS[0][1] * g
    for t in range(1, SWEEPS):
        momentum, step = WEIGHTS[t]
        for x in range(8):
            c, total = whole_around(t - 1, x)
            new = (1.0 + momentum - step) * c + step * (k3[9, x] + k3[5, x] * total)
            if t > 1:
                new = new - momentum * u3[t - 2, x]
            u3[t, x] = new
    for x in range(8):
        c, total = whole_around(3, x)
        r = (k3[8, x] - k3[0, x] * c) + 0.25**3 * total
        fold[32 * x : 32 * x + 32, :] = r + roll(r, 64, 1)
        for y in range(8):
            x3[x, y, 0:4, :] = c[4 * y : 4 * y + 4, :]
    value = fold[pl.ds(0, 128, stride=2), :] + fold[pl.ds(1, 128, stride=2), :]
    value = dot(value, picker("pair", 0, 32, 0, 0.125))
    o4[...] = value.reshape(8, 16, 128)[:, :, 0:32]
    mine = x3[gx, gy]
    for half in range(2):
        o3[half] = roll(mine, (128 - 64 * half) - 16 * gz, 1)[0:4, 0:16]
    sent(three_source)
    result.wait()


def hand_over(*refs):
    for k in range(5):
        refs[5 + k][...] = refs[k][...]


def body(*args):
    vm = lambda *shape: pltpu.VMEM(shape, F32)
    scratch = [
        vm(16, 32, 128), vm(16, 32, 128), vm(17, 32, 128), vm(16, 32, 128), vm(16, 32, 128),
        vm(16, 32, 128), vm(16, 32, 128), vm(16, 32, 128), vm(16, 32, 128), vm(16, 32, 128),
        vm(4, 18, 48, 128),
        vm(32, 128), vm(16, 128), vm(8, 128), vm(32, 128), vm(16, 128), vm(8, 128),
        vm(4, 2, 16, 128), vm(4, 2, 8, 128), vm(4, 2, 16, 128), vm(4, 8, 128),
        vm(256, 128), vm(256, 128),
        vm(2, 8, 16, 128), vm(4, 16, 128), vm(1, 8, 16, 128), vm(1, 16, 128),
        vm(2, 16, 24, 128), vm(4, 2, 3, 24, 128), vm(1, 16, 24, 128), vm(1, 2, 3, 24, 128),
        vm(10, 16, 24, 128), vm(4, 16, 24, 128),
        vm(4, 8, 128), vm(1, 8, 128), vm(3, 2, 4, 4, 8, 128), vm(3, 2, 4, 1, 8, 128),
        vm(10, 12, 16, 128), vm(4, 12, 16, 128),
        vm(2, 4, 4, 8, 4, 128), vm(4, 128), vm(8, 8, 4, 128), vm(11, 8, 32, 128), vm(4, 8, 32, 128),
        vm(8, 8, 8, 128),
        pltpu.SemaphoreType.DMA((5,)), pltpu.SemaphoreType.DMA,
        pltpu.SemaphoreType.DMA((288,)), pltpu.SemaphoreType.DMA((288,)),
    ]
    out = lambda *shape: jax.ShapeDtypeStruct(shape, F32)
    results = pl.pallas_call(
        kernel,
        out_shape=(out(16, 32, 128), out(8, 16, 64), out(4, 8, 32), out(2, 4, 16), out(8, 16, 32)),
        in_specs=[pl.BlockSpec(memory_space=pl.ANY)] * 5,
        out_specs=[pl.BlockSpec(memory_space=pl.ANY)] + [pl.BlockSpec(memory_space=pltpu.VMEM)] * 4,
        scratch_shapes=scratch,
        compiler_params=pltpu.CompilerParams(
            collective_id=0, has_side_effects=True, vmem_limit_bytes=63 * 2**20
        ),
    )(*args)
    return pl.pallas_call(
        hand_over,
        out_shape=tuple(out(*r.shape) for r in results),
        in_specs=[pl.BlockSpec(memory_space=pltpu.VMEM)] * 5,
        out_specs=[pl.BlockSpec(memory_space=pltpu.VMEM)] * 5,
    )(*results)


def solution(mesh):
    spec = P(*AXES)
    return jax.shard_map(
        body,
        mesh=mesh,
        in_specs=(spec,) * 5,
        out_specs=(spec, spec, spec, spec, P()),
        check_vma=False,
    )
```

```python
import itertools

import jax
import jax.numpy as jnp
from jax import lax
from jax.experimental import pallas as pl
from jax.experimental.pallas import tpu as pltpu
from jax.sharding import PartitionSpec as P

MESH = pl.DeviceIdType.MESH
AXES = ("gx", "gy", "gz")
SIZES = (8, 8, 4)
SWEEPS = 4
F32 = jnp.float32


def distance(d):
    return sum(min(s % n, -s % n) for s, n in zip(d, SIZES))


def farthest_first(xs, ys, zs):
    directions = [d for d in itertools.product(xs, ys, zs) if d != (0, 0, 0)]
    return tuple(sorted(directions, key=lambda d: -distance(d)))


BOX = farthest_first((-1, 0, 1), (-1, 0, 1), (-1, 0, 1))
COLUMNS = farthest_first((-1, 0, 1), (-1, 0, 1), (0, 1, 2, 3))
PLANE = farthest_first(range(8), range(8), (0,))
SIX = tuple(d for d in BOX if distance(d) == 1)

FACES, ROUND, ONE_C, ONE_S, TWO_C, TWO_S = 0, 1, 5, 6, 7, 8
THREE_X, THREE_Z, THREE_Y, THREE_CORE, THREE_S, GROUPS = 9, 10, 11, 12, 13, 14

FIELDS = (
    ("a", "pair", "pair", "pair"),
    ("bx", "even", "pair", "pair"),
    ("by", "pair", "even", "pair"),
    ("bz", "pair", "pair", "even"),
    ("hx", "odd", "pair", "pair"),
    ("hy", "pair", "odd", "pair"),
    ("hz", "pair", "pair", "odd"),
)


def chebyshev_weights(count):
    middle, spread = 1.125, 0.875
    sharpness = middle / spread
    weights = [(0.0, 1.0 / middle)]
    rho_prev = 1.0 / sharpness
    for _ in range(1, count):
        rho_next = 1.0 / (2.0 * sharpness - rho_prev)
        weights.append((rho_next * rho_prev, 2.0 * rho_next / spread))
        rho_prev = rho_next
    return weights


WEIGHTS = chebyshev_weights(SWEEPS)


def neighbour(d):
    return tuple(
        lax.rem(lax.axis_index(a) + ((s + n) % n), n) for a, s, n in zip(AXES, d, SIZES)
    )


def iota(shape, dim):
    return lax.broadcasted_iota(jnp.int32, shape, dim)


def roll(value, shift, axis):
    n = value.shape[axis]
    if isinstance(shift, int):
        shift %= n
        if shift == 0:
            return value
    return pltpu.roll(value, shift, axis)


def picker(mode, first, count, out):
    row = iota((128, 128), 0) - first
    col = iota((128, 128), 1) - out
    hit = (row >> 1) == col
    hit = hit & (col >= 0) & (col < count)
    if mode != "pair":
        hit = hit & ((row & 1) == (0 if mode == "even" else 1))
    return jnp.where(hit, 1.0, 0.0).astype(jnp.bfloat16)


def dot(value, matrix):
    high = value.astype(jnp.bfloat16)
    rest = value - high.astype(F32)
    middle = rest.astype(jnp.bfloat16)
    low = (rest - middle.astype(F32)).astype(jnp.bfloat16)
    parts = jnp.concatenate([high, middle, low], axis=1)
    return jnp.dot(parts, jnp.concatenate([matrix] * 3, axis=0), preferred_element_type=F32)


def x_pick(value, mode):
    n = value.shape[0]
    grouped = value.reshape((n // 2, 2) + value.shape[1:])
    if mode == "pair":
        return grouped[:, 0] + grouped[:, 1]
    return grouped[:, 0 if mode == "even" else 1]


def y_pick(tmp, value, mode):
    rows = value.shape[0]
    tmp[0:rows, :] = value
    if mode == "pair":
        return tmp[pl.ds(0, rows // 2, stride=2), :] + tmp[pl.ds(1, rows // 2, stride=2), :]
    return tmp[pl.ds(0 if mode == "even" else 1, rows // 2, stride=2), :]


def kernel(
    src_h, a_h, bx_h, by_h, bz_h,
    o0_h, o1, o2, o3, o4,
    src, a0, bx, by, bz, hy, hz, diag, inv_s, gain, v,
    send_fx, send_fy, send_fz, next_x, next_y, next_z,
    recv_y, recv_z, send_y, send_z,
    tmp, fold,
    s1c, p1c, s1s, p1s, r1c, q1c, r1s, q1s, k1, u1,
    s2c, s2s, r2c, r2s, k2, u2,
    r3, s3s, r3s, k3, u3, x3, gauge,
    in_sem, out_sem, send_sem, recv_sem,
):
    gx, gy, gz = (lax.axis_index(a) for a in AXES)
    rows = {}

    def push(group, source, target, d, device=None):
        n = 1
        for extent in target.shape[:-1]:
            n *= extent
        rows[group] = rows.get(group, 0) + n
        pltpu.make_async_remote_copy(
            src_ref=source,
            dst_ref=target,
            send_sem=send_sem.at[group],
            recv_sem=recv_sem.at[group],
            device_id=neighbour(d) if device is None else device,
            device_id_type=MESH,
        ).start()

    def wait(group, sem):
        measure = gauge.at[0 : rows[group]]
        pltpu.make_async_copy(measure, measure, sem.at[group]).wait()

    def received(group):
        wait(group, recv_sem)

    def sent(group):
        wait(group, send_sem)

    barrier = pltpu.get_barrier_semaphore()
    for d in SIX:
        pl.semaphore_signal(barrier, inc=1, device_id=neighbour(d), device_id_type=MESH)

    loads = []
    for k, (h, m) in enumerate(
        ((bx_h, bx.at[0:16]), (by_h, by), (bz_h, bz), (a_h, a0), (src_h, src))
    ):
        copy = pltpu.make_async_copy(h, m, in_sem.at[k])
        copy.start()
        loads.append(copy)
    for copy in loads:
        copy.wait()

    lane = iota((8, 128), 1)
    sub = iota((8, 128), 0)
    lane32 = iota((32, 128), 1)
    inner_x = jnp.where(gx > 0, 1.0, 0.0).astype(F32)
    inner_y = jnp.where(gy > 0, 1.0, 0.0).astype(F32)
    inner_z = jnp.where(gz > 0, 1.0, 0.0).astype(F32)

    def pack_ends(packed, value, x):
        for j in range(4):
            at = 32 * j + 2 * x
            moved = roll(value[8 * j : 8 * j + 8, :], at + 1, 1)
            packed = moved if packed is None else jnp.where((lane >> 1) == (at >> 1), moved, packed)
        return packed

    def unpack_ends(ends, x):
        return jnp.concatenate([roll(ends, -(32 * j + 2 * x + 1), 1) for j in range(4)], axis=0)

    send_fx[...] = bx[0] * inner_x
    packed = None
    for x in range(16):
        send_fy[x : x + 1, :] = by[x, 0:1, :] * inner_y
        packed = pack_ends(packed, bz[x], x)
    send_fz[...] = packed * inner_z

    SHAPES = {1: (16, 32), 2: (8, 16), 3: (4, 8)}
    LANES = {1: (0, 64, 64), 2: (64, 32, 0), 3: (0, 16, 0)}
    OWN = {1: {}, 2: {}, 3: {}}

    def coarsen(level, names, fine):
        first, count, out = LANES[level]
        n, m = SHAPES[level]
        size = n * m // 4
        groups = {"pair": [], "even": []}
        for k, (name, xm, ym, zm) in enumerate(FIELDS):
            if name not in names:
                continue
            value = y_pick(tmp, x_pick(fine(name), xm).reshape(n // 2 * m, 128), ym)
            if zm == "odd":
                value = roll(value, -1, 1)
            groups["pair" if zm == "pair" else "even"].append((k, name, value))
        for zm, members in groups.items():
            value = jnp.concatenate([part for _, _, part in members], axis=0)
            value = dot(value, picker(zm, first, count, out))
            for at, (k, name, _) in enumerate(members):
                part = value[at * size : (at + 1) * size, :]
                OWN[level][k] = part * (0.125 if name == "a" else 0.25)

    INDEX = {f[0]: k for k, f in enumerate(FIELDS)}

    def own(level):
        n, m = SHAPES[level + 1] if level < 3 else (2, 4)
        return lambda name: OWN[level][INDEX[name]].reshape(n, m, 128)

    fine = {"a": a0, "by": by, "bz": bz, "hy": hy, "hz": hz}

    def level_zero(name):
        if name == "bx":
            return bx[0:16]
        if name == "hx":
            return bx[1:17]
        return fine[name][...]

    low = ("a", "bx", "by", "bz")
    high = ("hx", "hy", "hz")

    coarsen(1, low, level_zero)
    coarsen(2, low, own(1))
    coarsen(3, low, own(2))

    pl.semaphore_wait(barrier, 6)

    push(FACES, send_fx, next_x, (-1, 0, 0))
    push(FACES, send_fy, next_y, (0, -1, 0))
    push(FACES, send_fz, next_z, (0, 0, -1))

    def swap_lanes(from_low, from_high):
        odd = (lane & 1) == 1
        return jnp.where(odd, roll(from_low, 1, 1), roll(from_high, -1, 1))

    ORDER = (0, 15) + tuple(range(1, 15))

    def exchange_x(t):
        push(ROUND + t, v.at[t, 1, 8:40], v.at[t, 17, 8:40], (-1, 0, 0))
        push(ROUND + t, v.at[t, 16, 8:40], v.at[t, 0, 8:40], (1, 0, 0))

    def exchange_yz(t):
        for x in range(16):
            send_y[t, 0, x : x + 1, :] = v[t, 1 + x, 8:9, :]
            send_y[t, 1, x : x + 1, :] = v[t, 1 + x, 39:40, :]
        push(ROUND + t, send_z.at[t], recv_z.at[t, 1], (0, 0, -1))
        push(ROUND + t, send_z.at[t], recv_z.at[t, 0], (0, 0, 1))
        push(ROUND + t, send_y.at[t, 0], recv_y.at[t, 1], (0, -1, 0))
        push(ROUND + t, send_y.at[t, 1], recv_y.at[t, 0], (0, 1, 0))

    def land(t):
        for x in range(16):
            v[t, 1 + x, 7:8, :] = recv_y[t, 0, x : x + 1, :]
            v[t, 1 + x, 40:41, :] = recv_y[t, 1, x : x + 1, :]
        return swap_lanes(recv_z[t, 0], recv_z[t, 1])

    def around(t, x, ends):
        c = v[t, 1 + x, 8:40, :]
        halo = unpack_ends(ends, x)
        below = jnp.where(lane32 == 0, halo, roll(c, 1, 1))
        above = jnp.where(lane32 == 127, halo, roll(c, -1, 1))
        total = bx[x] * v[t, x, 8:40, :] + bx[x + 1] * v[t, x + 2, 8:40, :]
        total = total + (by[x] * v[t, 1 + x, 7:39, :] + hy[x] * v[t, 1 + x, 9:41, :])
        return c, total + (bz[x] * below + hz[x] * above)

    received(FACES)
    bx[16] = next_x[...]
    ends = roll(next_z[...], -1, 1)
    packed = None
    row32 = iota((32, 128), 0)
    for x in ORDER:
        b = by[x]
        up = jnp.where(row32 == 31, jnp.broadcast_to(next_y[x : x + 1, :], (32, 128)), roll(b, -1, 0))
        hy[x] = up
        total = (bx[x] + bx[x + 1]) + (b + up)
        b = bz[x]
        halo = jnp.concatenate([roll(ends, -(32 * j + 2 * x + 1), 1) for j in range(4)], axis=0)
        up = jnp.where(lane32 == 127, halo, roll(b, -1, 1))
        hz[x] = up
        total = a0[x] + (total + (b + up))
        diag[x] = total
        inverse = 1.0 / total
        inv_s[x] = inverse
        g = inverse * src[x]
        gain[x] = g
        g = g * WEIGHTS[0][1]
        v[0, 1 + x, 8:40, :] = g
        packed = pack_ends(packed, g, x)
        if x == 15:
            exchange_x(0)
    send_z[0] = packed
    exchange_yz(0)

    coarsen(1, high, level_zero)
    coarsen(2, high, own(1))
    coarsen(3, high, own(2))
    bx[0] = bx[0] * inner_x
    for x in range(16):
        by[x, 0:1, :] = by[x, 0:1, :] * inner_y
        bz[x] = jnp.where(lane32 == 0, bz[x] * inner_z, bz[x])

    def own_coefficients(level):
        scale = 0.25**level
        get = OWN[level]
        a, lx, ly, lz, ux, uy, uz = (get[k] for k in range(7))
        d = a + scale * ((lx + ux) + (ly + uy) + (lz + uz))
        rows = d.shape[0]
        row = iota((rows, 128), 0)
        m = SHAPES[level][1] // 2
        first = LANES[level][2]
        lx = jnp.where(row < m, lx * inner_x, lx)
        ly = jnp.where((row & (m - 1)) == 0, ly * inner_y, ly)
        lz = jnp.where(iota((rows, 128), 1) == first, lz * inner_z, lz)
        return d, lx, ly, lz

    def pack_one(value):
        lane16 = iota((16, 128), 1) >> 2
        packed = None
        for x in range(8):
            moved = roll(value[16 * x : 16 * x + 16, :], 4 * x + 4, 1)
            if packed is None:
                packed = moved
            else:
                packed = jnp.where((lane16 == x) | (lane16 == x + 17), moved, packed)
        return packed

    def send_one(group, s, p, r, q, reach):
        for d in BOX:
            if distance(d) not in reach:
                continue
            dx, dy, dz = d
            xs = {0: pl.ds(0, 8), 1: pl.ds(4, 4), -1: pl.ds(0, 4)}[dx]
            xd = {0: pl.ds(4, 8), 1: pl.ds(0, 4), -1: pl.ds(12, 4)}[dx]
            ys = {0: pl.ds(0, 16), 1: pl.ds(12, 4), -1: pl.ds(0, 4)}[dy]
            yd = {0: pl.ds(0, 16), 1: pl.ds(20, 4), -1: pl.ds(16, 4)}[dy]
            if dz == 0:
                push(group, s.at[:, xs, ys], r.at[:, xd, yd], d)
            else:
                push(group, p.at[:, ys], q.at[:, 0 if dz == 1 else 1, 1 - dx, yd], d)

    lane24 = iota((24, 128), 1)

    def assemble_one(get, q, f, out):
        for b, (start, rows) in enumerate(((0, range(4, 8)), (4, range(8)), (12, range(4)))):
            m = jnp.where(lane24 < 64, q[f, 0, b], q[f, 1, b])
            for n, xl in enumerate(rows):
                out[start + n] = jnp.where(lane24 >= 64, get(start + n), roll(m, 60 - 4 * xl, 1))

    fields = own_coefficients(1)
    for f, value in enumerate(fields):
        p1c[f] = pack_one(value)
    for f in range(2):
        value = (fields[2 * f] + roll(fields[2 * f + 1], 64, 1)).reshape(8, 16, 128)
        s1c[f] = value
        r1c[f, 4:12, 0:16, :] = value
    send_one(ONE_C, s1c, p1c, r1c, q1c, (1,))

    def pack_two(value):
        packed = value[0:8, :]
        for x in range(1, 4):
            packed = packed + roll(value[8 * x : 8 * x + 8, :], 32 * x, 1)
        return packed

    def send_two(group, s, r, reach):
        for d in COLUMNS:
            if distance(d) not in reach:
                continue
            target = r.at[1 - d[0], 1 if d[1] else 0, gz]
            if d[1] == 0:
                push(group, s, target, d)
            else:
                half = pl.ds(4, 4) if d[1] == 1 else pl.ds(0, 4)
                push(group, s.at[:, half], target.at[:, half], d)

    def assemble_two(get, out):
        for b in range(3):
            for t in range(2):
                tiles = [get(b, t, z) for z in range(4)]
                for x in range(4):
                    value = roll(tiles[0], -32 * x, 1)
                    for z in range(1, 4):
                        value = jnp.where((lane >> 5) == z, roll(tiles[z], 32 * (z - x), 1), value)
                    out[4 * b + x, 8 * t : 8 * t + 8, :] = value

    def sweep(t):
        momentum, step = WEIGHTS[t + 1]
        ends = land(t)
        packed = None
        for x in ORDER:
            c, total = around(t, x, ends)
            new = (1.0 + momentum - step) * c + step * (gain[x] + inv_s[x] * total)
            if t > 0:
                new = new - momentum * v[t - 1, 1 + x, 8:40, :]
            v[t + 1, 1 + x, 8:40, :] = new
            packed = pack_ends(packed, new, x)
            if x == 15:
                exchange_x(t + 1)
        send_z[t + 1] = packed
        exchange_yz(t + 1)

    sent(FACES)
    received(ROUND + 0)
    sweep(0)

    send_one(ONE_C, s1c, p1c, r1c, q1c, (2,))
    for f, value in enumerate(own_coefficients(2)):
        s2c[f] = pack_two(value)
    r2c[1, 0, gz] = s2c[...]
    halves_of = lambda value: jnp.where(sub < 4, value, roll(value, 64, 1))
    total = None
    for f, value in enumerate(own_coefficients(3)):
        halves = halves_of(value)
        halves = roll(halves + roll(halves, 4, 0), 16 * f, 1)
        total = halves if total is None else total + halves
    parity, chip = gy % 2, gy // 2
    r3[parity, chip, gz, gx] = total[0:4, :]

    sent(ROUND + 0)
    received(ROUND + 1)
    sweep(1)
    send_one(ONE_C, s1c, p1c, r1c, q1c, (3,))
    send_two(TWO_C, s2c, r2c, (1, 2, 3))

    def prepare(k, planes, scale):
        for x in range(planes):
            d = k[0, x]
            inverse = 1.0 / jnp.where(d > 0, d, 1.0)
            k[4, x] = inverse
            k[5, x] = scale * inverse
            k[6, x] = roll(k[2, x], -1, 0)
            k[7, x] = roll(k[3, x], -1, 1)

    sent(ROUND + 1)
    received(ROUND + 2)
    sweep(2)
    send_two(TWO_C, s2c, r2c, (4,))
    block = r3.at[parity, chip, gz, gx]
    for d in (4, 3, 5, 2, 6, 1, 7):
        push(THREE_X, block, block, (d, 0, 0))

    result = pltpu.make_async_copy(v.at[3, 1:17, 8:40], o0_h, out_sem)
    result.start()

    received(ONE_C)
    for f in range(4):
        if f % 2 == 0:
            assemble_one(lambda x, f=f: r1c[f // 2, x], q1c, f, k1.at[f])
        else:
            assemble_one(lambda x, f=f: roll(r1c[f // 2, x], 64, 1), q1c, f, k1.at[f])
    prepare(k1, 16, 0.25)
    sent(ONE_C)
    sent(ROUND + 2)
    received(ROUND + 3)

    ends = land(3)
    for x in range(0, 16, 2):
        pair = None
        for y in (x, x + 1):
            c, total = around(3, y, ends)
            r = (src[y] - diag[y] * c) + total
            pair = r if pair is None else pair + r
        fold[16 * x : 16 * x + 32, :] = pair
    value = fold[pl.ds(0, 128, stride=2), :] + fold[pl.ds(1, 128, stride=2), :]
    value = dot(value, picker("pair", 0, 64, 64)) * 0.125
    s1s[0] = value.reshape(8, 16, 128)
    r1s[0, 4:12, 0:16, :] = s1s[0]
    p1s[0] = pack_one(value)
    send_one(ONE_S, s1s, p1s, r1s, q1s, (1, 2, 3))

    received(THREE_X)
    block = r3.at[parity, chip, gz]
    for d in (2, 1, 3):
        push(THREE_Z, block, block, (0, 0, d))
    received(TWO_C)
    for f in range(4):
        assemble_two(lambda b, t, z, f=f: r2c[b, t, z, f], k2.at[f])
    prepare(k2, 12, 0.25**2)
    sent(TWO_C)
    sent(THREE_X)
    received(THREE_Z)
    block = r3.at[parity, chip]
    for d in (4, 2, 6):
        push(THREE_Y, block, block, (0, d, 0))
    sent(ROUND + 3)
    received(ONE_S)

    def wide_around(k, c, lower, upper, x):
        total = k[1, x] * lower + k[1, x + 1] * upper
        total = total + (k[2, x] * roll(c, 1, 0) + k[6, x] * roll(c, -1, 0))
        return total + (k[3, x] * roll(c, 1, 1) + k[7, x] * roll(c, -1, 1))

    def wide_level(k, u, planes):
        for x in range(planes):
            g = k[4, x] * k[8, x]
            k[9, x] = g
            u[0, x] = WEIGHTS[0][1] * g
        for t in range(1, SWEEPS):
            momentum, step = WEIGHTS[t]
            for x in range(t, planes - t):
                c = u[t - 1, x]
                total = wide_around(k, c, u[t - 1, x - 1], u[t - 1, x + 1], x)
                new = (1.0 + momentum - step) * c + step * (k[9, x] + k[5, x] * total)
                if t > 1:
                    new = new - momentum * u[t - 2, x]
                u[t, x] = new

    def wide_residual(k, u, x, scale):
        c = u[3, x]
        total = wide_around(k, c, u[3, x - 1], u[3, x + 1], x)
        return (k[8, x] - k[0, x] * c) + scale * total

    assemble_one(lambda x: r1s[0, x], q1s, 0, k1.at[8])
    wide_level(k1, u1, 16)
    lane16 = iota((16, 128), 1)
    for x in range(4):
        r = wide_residual(k1, u1, 4 + 2 * x, 0.25) + wide_residual(k1, u1, 5 + 2 * x, 0.25)
        fold[16 * x : 16 * x + 16, :] = jnp.where(lane16 >= 64, r[0:16, :], 0.0)
    value = fold[pl.ds(0, 32, stride=2), :] + fold[pl.ds(1, 32, stride=2), :]
    value = dot(value, picker("pair", 64, 32, 0)) * 0.125
    s2s[0] = pack_two(value)
    r2s[1, 0, gz] = s2s[...]
    send_two(TWO_S, s2s, r2s, (1, 2, 3, 4))
    sent(THREE_Z)
    received(THREE_Y)
    block = r3.at[parity]
    push(THREE_CORE, block, block, None, (gx, gy + 1 - 2 * parity, gz))
    for x in range(8):
        o1[x] = roll(u1[3, 4 + x, 0:16, :], 64, 1)[:, 0:64]
    received(THREE_CORE)
    group = (lane >> 4) & 3
    for x in range(8):
        for p in range(4):
            tiles = [jnp.concatenate([r3[0, p, z, x], r3[1, p, z, x]], axis=0) for z in range(4)]
            for f in range(4):
                value = roll(tiles[0], -16 * f, 1)
                for z in range(1, 4):
                    value = jnp.where(group == z, roll(tiles[z], 16 * (z - f), 1), value)
                k3[f, x, 8 * p : 8 * p + 8, :] = value
    lane8 = iota((32, 128), 1)
    for x in range(8):
        inverse = 1.0 / k3[0, x]
        k3[4, x] = inverse
        k3[5, x] = 0.25**3 * inverse
        k3[6, x] = roll(k3[2, x], -1, 0)
        k3[7, x] = roll(k3[3, x], -1, 1)
        here, after = roll(k3[1, x], 64, 1), roll(k3[1, (x + 1) % 8], 64, 1)
        k3[10, x] = jnp.where(lane8 < 64, here, after)
    sent(ONE_S)
    sent(THREE_Y)
    received(TWO_S)

    assemble_two(lambda b, t, z: r2s[b, t, z, 0], k2.at[8])
    wide_level(k2, u2, 12)
    for x in range(2):
        r = wide_residual(k2, u2, 4 + 2 * x, 0.25**2) + wide_residual(k2, u2, 5 + 2 * x, 0.25**2)
        fold[8 * x : 8 * x + 8, :] = r[0:8, :]
    value = fold[pl.ds(0, 8, stride=2), :] + fold[pl.ds(1, 8, stride=2), :]
    value = dot(value, picker("pair", 0, 64, 0)) * 0.125
    halves = halves_of(value)
    s3s[...] = (halves + roll(halves, 4, 0))[0:4, :]
    r3s[gx, gy] = s3s[...]
    for d in PLANE:
        push(THREE_S, s3s, r3s.at[gx, gy], d)
    for x in range(4):
        o2[x] = roll(u2[3, 4 + x, 0:8, :], 128 - 32 * gz, 1)[:, 0:32]
    sent(TWO_S)
    sent(THREE_CORE)
    received(THREE_S)

    for y in range(8):
        k3[8, :, 4 * y : 4 * y + 4, :] = r3s[:, y]

    def whole_around(t, x):
        c = u3[t, x]
        turned = roll(c, 64, 1)
        lower = jnp.where(lane8 < 64, roll(u3[t, (x + 7) % 8], 64, 1), turned)
        upper = jnp.where(lane8 < 64, turned, roll(u3[t, (x + 1) % 8], 64, 1))
        total = k3[1, x] * lower + k3[10, x] * upper
        total = total + (k3[2, x] * roll(c, 1, 0) + k3[6, x] * roll(c, -1, 0))
        return c, total + (k3[3, x] * roll(c, 1, 1) + k3[7, x] * roll(c, -1, 1))

    for x in range(8):
        g = k3[4, x] * k3[8, x]
        k3[9, x] = g
        u3[0, x] = WEIGHTS[0][1] * g
    for t in range(1, SWEEPS):
        momentum, step = WEIGHTS[t]
        for x in range(8):
            c, total = whole_around(t - 1, x)
            new = (1.0 + momentum - step) * c + step * (k3[9, x] + k3[5, x] * total)
            if t > 1:
                new = new - momentum * u3[t - 2, x]
            u3[t, x] = new
    for x in range(8):
        c, total = whole_around(3, x)
        r = (k3[8, x] - k3[0, x] * c) + 0.25**3 * total
        fold[32 * x : 32 * x + 32, :] = r + roll(r, 64, 1)
        for y in range(8):
            x3[x, y, 0:4, :] = c[4 * y : 4 * y + 4, :]
    value = fold[pl.ds(0, 128, stride=2), :] + fold[pl.ds(1, 128, stride=2), :]
    value = dot(value, picker("pair", 0, 32, 0)) * 0.125
    o4[...] = value.reshape(8, 16, 128)[:, :, 0:32]
    mine = x3[gx, gy]
    for half in range(2):
        o3[half] = roll(mine, (128 - 64 * half) - 16 * gz, 1)[0:4, 0:16]
    sent(THREE_S)
    result.wait()


def hand_over(*refs):
    for k in range(5):
        refs[5 + k][...] = refs[k][...]


def body(*args):
    vm = lambda *shape: pltpu.VMEM(shape, F32)
    scratch = [
        vm(16, 32, 128), vm(16, 32, 128), vm(17, 32, 128), vm(16, 32, 128), vm(16, 32, 128),
        vm(16, 32, 128), vm(16, 32, 128), vm(16, 32, 128), vm(16, 32, 128), vm(16, 32, 128),
        vm(4, 18, 48, 128),
        vm(32, 128), vm(16, 128), vm(8, 128), vm(32, 128), vm(16, 128), vm(8, 128),
        vm(4, 2, 16, 128), vm(4, 2, 8, 128), vm(4, 2, 16, 128), vm(4, 8, 128),
        vm(256, 128), vm(256, 128),
        vm(2, 8, 16, 128), vm(4, 16, 128), vm(1, 8, 16, 128), vm(1, 16, 128),
        vm(2, 16, 24, 128), vm(4, 2, 3, 24, 128), vm(1, 16, 24, 128), vm(1, 2, 3, 24, 128),
        vm(10, 16, 24, 128), vm(4, 16, 24, 128),
        vm(4, 8, 128), vm(1, 8, 128), vm(3, 2, 4, 4, 8, 128), vm(3, 2, 4, 1, 8, 128),
        vm(10, 12, 16, 128), vm(4, 12, 16, 128),
        vm(2, 4, 4, 8, 4, 128), vm(4, 128), vm(8, 8, 4, 128), vm(11, 8, 32, 128), vm(4, 8, 32, 128),
        vm(8, 8, 8, 128), vm(2048, 128),
        pltpu.SemaphoreType.DMA((5,)), pltpu.SemaphoreType.DMA,
        pltpu.SemaphoreType.DMA((GROUPS,)), pltpu.SemaphoreType.DMA((GROUPS,)),
    ]
    out = lambda *shape: jax.ShapeDtypeStruct(shape, F32)
    results = pl.pallas_call(
        kernel,
        out_shape=(out(16, 32, 128), out(8, 16, 64), out(4, 8, 32), out(2, 4, 16), out(8, 16, 32)),
        in_specs=[pl.BlockSpec(memory_space=pl.ANY)] * 5,
        out_specs=[pl.BlockSpec(memory_space=pl.ANY)] + [pl.BlockSpec(memory_space=pltpu.VMEM)] * 4,
        scratch_shapes=scratch,
        compiler_params=pltpu.CompilerParams(
            collective_id=0, has_side_effects=True, vmem_limit_bytes=63 * 2**20
        ),
    )(*args)
    return pl.pallas_call(
        hand_over,
        out_shape=tuple(out(*r.shape) for r in results),
        in_specs=[pl.BlockSpec(memory_space=pltpu.VMEM)] * 5,
        out_specs=[pl.BlockSpec(memory_space=pltpu.VMEM)] * 5,
    )(*results)


def solution(mesh):
    spec = P(*AXES)
    return jax.shard_map(
        body,
        mesh=mesh,
        in_specs=(spec,) * 5,
        out_specs=(spec, spec, spec, spec, P()),
        check_vma=False,
    )
```

```python
import itertools

import jax
import jax.numpy as jnp
from jax import lax
from jax.experimental import pallas as pl
from jax.experimental.pallas import tpu as pltpu
from jax.sharding import PartitionSpec as P

MESH = pl.DeviceIdType.MESH
AXES = ("gx", "gy", "gz")
SIZES = (8, 8, 4)
SWEEPS = 4
F32 = jnp.float32


def distance(d):
    return sum(min(s % n, -s % n) for s, n in zip(d, SIZES))


def farthest_first(xs, ys, zs):
    directions = [d for d in itertools.product(xs, ys, zs) if d != (0, 0, 0)]
    return tuple(sorted(directions, key=lambda d: -distance(d)))


BOX = farthest_first((-1, 0, 1), (-1, 0, 1), (-1, 0, 1))
COLUMNS = farthest_first((-1, 0, 1), (-1, 0, 1), (0, 1, 2, 3))
PLANE = farthest_first(range(8), range(8), (0,))
SIX = tuple(d for d in BOX if distance(d) == 1)

FACES, ROUND, ONE_C, ONE_S, TWO_C, TWO_S = 0, 1, 5, 6, 7, 8
THREE_X, THREE_Z, THREE_Y, THREE_CORE, THREE_S, GROUPS = 9, 10, 11, 12, 13, 14

FIELDS = (
    ("a", "pair", "pair", "pair"),
    ("bx", "even", "pair", "pair"),
    ("by", "pair", "even", "pair"),
    ("bz", "pair", "pair", "even"),
    ("hx", "odd", "pair", "pair"),
    ("hy", "pair", "odd", "pair"),
    ("hz", "pair", "pair", "odd"),
)


def chebyshev_weights(count):
    middle, spread = 1.125, 0.875
    sharpness = middle / spread
    weights = [(0.0, 1.0 / middle)]
    rho_prev = 1.0 / sharpness
    for _ in range(1, count):
        rho_next = 1.0 / (2.0 * sharpness - rho_prev)
        weights.append((rho_next * rho_prev, 2.0 * rho_next / spread))
        rho_prev = rho_next
    return weights


WEIGHTS = chebyshev_weights(SWEEPS)


def neighbour(d):
    return tuple(
        lax.rem(lax.axis_index(a) + ((s + n) % n), n) for a, s, n in zip(AXES, d, SIZES)
    )


def iota(shape, dim):
    return lax.broadcasted_iota(jnp.int32, shape, dim)


def roll(value, shift, axis):
    n = value.shape[axis]
    if isinstance(shift, int):
        shift %= n
        if shift == 0:
            return value
    return pltpu.roll(value, shift, axis)


def picker(mode, first, count, out):
    row = iota((128, 128), 0) - first
    col = iota((128, 128), 1) - out
    hit = (row >> 1) == col
    hit = hit & (col >= 0) & (col < count)
    if mode != "pair":
        hit = hit & ((row & 1) == (0 if mode == "even" else 1))
    return jnp.where(hit, 1.0, 0.0).astype(jnp.bfloat16)


def dot(value, matrix):
    high = value.astype(jnp.bfloat16)
    rest = value - high.astype(F32)
    middle = rest.astype(jnp.bfloat16)
    low = (rest - middle.astype(F32)).astype(jnp.bfloat16)
    parts = jnp.concatenate([high, middle, low], axis=1)
    return jnp.dot(parts, jnp.concatenate([matrix] * 3, axis=0), preferred_element_type=F32)


def x_pick(value, mode):
    n = value.shape[0]
    grouped = value.reshape((n // 2, 2) + value.shape[1:])
    if mode == "pair":
        return grouped[:, 0] + grouped[:, 1]
    return grouped[:, 0 if mode == "even" else 1]


def y_pick(tmp, value, mode):
    rows = value.shape[0]
    tmp[0:rows, :] = value
    if mode == "pair":
        return tmp[pl.ds(0, rows // 2, stride=2), :] + tmp[pl.ds(1, rows // 2, stride=2), :]
    return tmp[pl.ds(0 if mode == "even" else 1, rows // 2, stride=2), :]


def kernel(
    src_h, a_h, bx_h, by_h, bz_h,
    o0_h, o1, o2, o3, o4,
    src, a0, bx, by, bz, hy, hz, diag, inv_s, gain, v,
    send_fx, send_fy, send_fz, next_x, next_y, next_z,
    recv_y, recv_z, send_y, send_z,
    tmp, fold,
    s1c, p1c, s1s, p1s, r1c, q1c, r1s, q1s, k1, u1,
    s2c, s2s, r2c, r2s, k2, u2,
    r3, s3s, r3s, k3, u3, x3, gauge,
    in_sem, out_sem, send_sem, recv_sem,
):
    gx, gy, gz = (lax.axis_index(a) for a in AXES)
    rows = {}

    def push(group, source, target, d, device=None):
        n = 1
        for extent in target.shape[:-1]:
            n *= extent
        rows[group] = rows.get(group, 0) + n
        pltpu.make_async_remote_copy(
            src_ref=source,
            dst_ref=target,
            send_sem=send_sem.at[group],
            recv_sem=recv_sem.at[group],
            device_id=neighbour(d) if device is None else device,
            device_id_type=MESH,
        ).start()

    def wait(group, sem):
        measure = gauge.at[0 : rows[group]]
        pltpu.make_async_copy(measure, measure, sem.at[group]).wait()

    def received(group):
        wait(group, recv_sem)

    def sent(group):
        wait(group, send_sem)

    barrier = pltpu.get_barrier_semaphore()
    for d in SIX:
        pl.semaphore_signal(barrier, inc=1, device_id=neighbour(d), device_id_type=MESH)

    loads = []
    for k, (h, m) in enumerate(
        ((bx_h, bx.at[0:16]), (by_h, by), (bz_h, bz), (a_h, a0), (src_h, src))
    ):
        copy = pltpu.make_async_copy(h, m, in_sem.at[k])
        copy.start()
        loads.append(copy)
    for copy in loads:
        copy.wait()

    lane = iota((8, 128), 1)
    sub = iota((8, 128), 0)
    lane32 = iota((32, 128), 1)
    inner_x = jnp.where(gx > 0, 1.0, 0.0).astype(F32)
    inner_y = jnp.where(gy > 0, 1.0, 0.0).astype(F32)
    inner_z = jnp.where(gz > 0, 1.0, 0.0).astype(F32)

    def pack_ends(packed, value, x):
        for j in range(4):
            at = 32 * j + 2 * x
            moved = roll(value[8 * j : 8 * j + 8, :], at + 1, 1)
            packed = moved if packed is None else jnp.where((lane >> 1) == (at >> 1), moved, packed)
        return packed

    def unpack_ends(ends, x):
        return jnp.concatenate([roll(ends, -(32 * j + 2 * x + 1), 1) for j in range(4)], axis=0)

    send_fx[...] = bx[0] * inner_x
    packed = None
    for x in range(16):
        send_fy[x : x + 1, :] = by[x, 0:1, :] * inner_y
        packed = pack_ends(packed, bz[x], x)
    send_fz[...] = packed * inner_z

    zeros = jnp.zeros((32, 128), F32)
    v[3, 0, 8:40, :] = zeros
    v[3, 17, 8:40, :] = zeros
    for x in range(16):
        v[3, 1 + x, 7:8, :] = zeros[0:1, :]
        v[3, 1 + x, 40:41, :] = zeros[0:1, :]
    for e in range(10):
        s1s[e] = zeros[0:24, :]

    SHAPES = {1: (16, 32), 2: (8, 16), 3: (4, 8)}
    LANES = {1: (0, 64, 64), 2: (64, 32, 0), 3: (0, 16, 0)}
    OWN = {1: {}, 2: {}, 3: {}}

    def coarsen(level, names, fine):
        first, count, out = LANES[level]
        n, m = SHAPES[level]
        size = n * m // 4
        groups = {"pair": [], "even": []}
        for k, (name, xm, ym, zm) in enumerate(FIELDS):
            if name not in names:
                continue
            value = y_pick(tmp, x_pick(fine(name), xm).reshape(n // 2 * m, 128), ym)
            if zm == "odd":
                value = roll(value, -1, 1)
            groups["pair" if zm == "pair" else "even"].append((k, name, value))
        for zm, members in groups.items():
            value = jnp.concatenate([part for _, _, part in members], axis=0)
            value = dot(value, picker(zm, first, count, out))
            for at, (k, name, _) in enumerate(members):
                part = value[at * size : (at + 1) * size, :]
                OWN[level][k] = part * (0.125 if name == "a" else 0.25)

    INDEX = {f[0]: k for k, f in enumerate(FIELDS)}

    def own(level):
        n, m = SHAPES[level + 1] if level < 3 else (2, 4)
        return lambda name: OWN[level][INDEX[name]].reshape(n, m, 128)

    fine = {"a": a0, "by": by, "bz": bz, "hy": hy, "hz": hz}

    def level_zero(name):
        if name == "bx":
            return bx[0:16]
        if name == "hx":
            return bx[1:17]
        return fine[name][...]

    low = ("a", "bx", "by", "bz")
    high = ("hx", "hy", "hz")

    coarsen(1, low, level_zero)
    coarsen(2, low, own(1))
    coarsen(3, low, own(2))

    pl.semaphore_wait(barrier, 6)

    push(FACES, send_fx, next_x, (-1, 0, 0))
    push(FACES, send_fy, next_y, (0, -1, 0))
    push(FACES, send_fz, next_z, (0, 0, -1))

    def swap_lanes(from_low, from_high):
        odd = (lane & 1) == 1
        return jnp.where(odd, roll(from_low, 1, 1), roll(from_high, -1, 1))

    ORDER = (0, 15) + tuple(range(1, 15))

    def exchange_x(t):
        push(ROUND + t, v.at[t, 1, 8:40], v.at[t, 17, 8:40], (-1, 0, 0))
        push(ROUND + t, v.at[t, 16, 8:40], v.at[t, 0, 8:40], (1, 0, 0))

    def exchange_yz(t):
        for x in range(16):
            send_y[t, 0, x : x + 1, :] = v[t, 1 + x, 8:9, :]
            send_y[t, 1, x : x + 1, :] = v[t, 1 + x, 39:40, :]
        push(ROUND + t, send_z.at[t], recv_z.at[t, 1], (0, 0, -1))
        push(ROUND + t, send_z.at[t], recv_z.at[t, 0], (0, 0, 1))
        push(ROUND + t, send_y.at[t, 0], recv_y.at[t, 1], (0, -1, 0))
        push(ROUND + t, send_y.at[t, 1], recv_y.at[t, 0], (0, 1, 0))

    def land(t):
        for x in range(16):
            v[t, 1 + x, 7:8, :] = recv_y[t, 0, x : x + 1, :]
            v[t, 1 + x, 40:41, :] = recv_y[t, 1, x : x + 1, :]
        return swap_lanes(recv_z[t, 0], recv_z[t, 1])

    def around(t, x, ends):
        c = v[t, 1 + x, 8:40, :]
        halo = 0.0 if ends is None else unpack_ends(ends, x)
        below = jnp.where(lane32 == 0, halo, roll(c, 1, 1))
        above = jnp.where(lane32 == 127, halo, roll(c, -1, 1))
        total = bx[x] * v[t, x, 8:40, :] + bx[x + 1] * v[t, x + 2, 8:40, :]
        total = total + (by[x] * v[t, 1 + x, 7:39, :] + hy[x] * v[t, 1 + x, 9:41, :])
        return c, total + (bz[x] * below + hz[x] * above)

    received(FACES)
    bx[16] = next_x[...]
    ends = roll(next_z[...], -1, 1)
    packed = None
    row32 = iota((32, 128), 0)
    for x in ORDER:
        b = by[x]
        up = jnp.where(row32 == 31, jnp.broadcast_to(next_y[x : x + 1, :], (32, 128)), roll(b, -1, 0))
        hy[x] = up
        total = (bx[x] + bx[x + 1]) + (b + up)
        b = bz[x]
        halo = jnp.concatenate([roll(ends, -(32 * j + 2 * x + 1), 1) for j in range(4)], axis=0)
        up = jnp.where(lane32 == 127, halo, roll(b, -1, 1))
        hz[x] = up
        total = a0[x] + (total + (b + up))
        diag[x] = total
        inverse = 1.0 / total
        inv_s[x] = inverse
        g = inverse * src[x]
        gain[x] = g
        g = g * WEIGHTS[0][1]
        v[0, 1 + x, 8:40, :] = g
        packed = pack_ends(packed, g, x)
        if x == 15:
            exchange_x(0)
    send_z[0] = packed
    exchange_yz(0)

    coarsen(1, high, level_zero)
    coarsen(2, high, own(1))
    coarsen(3, high, own(2))
    bx[0] = bx[0] * inner_x
    for x in range(16):
        by[x, 0:1, :] = by[x, 0:1, :] * inner_y
        bz[x] = jnp.where(lane32 == 0, bz[x] * inner_z, bz[x])

    def own_coefficients(level):
        scale = 0.25**level
        get = OWN[level]
        a, lx, ly, lz, ux, uy, uz = (get[k] for k in range(7))
        d = a + scale * ((lx + ux) + (ly + uy) + (lz + uz))
        rows = d.shape[0]
        row = iota((rows, 128), 0)
        m = SHAPES[level][1] // 2
        first = LANES[level][2]
        lx = jnp.where(row < m, lx * inner_x, lx)
        ly = jnp.where((row & (m - 1)) == 0, ly * inner_y, ly)
        lz = jnp.where(iota((rows, 128), 1) == first, lz * inner_z, lz)
        return d, lx, ly, lz

    def pack_one(value):
        lane16 = iota((16, 128), 1) >> 2
        packed = None
        for x in range(8):
            moved = roll(value[16 * x : 16 * x + 16, :], 4 * x + 4, 1)
            if packed is None:
                packed = moved
            else:
                packed = jnp.where((lane16 == x) | (lane16 == x + 17), moved, packed)
        return packed

    def send_one(group, s, p, r, q, reach):
        for d in BOX:
            if distance(d) not in reach:
                continue
            dx, dy, dz = d
            xs = {0: pl.ds(0, 8), 1: pl.ds(4, 4), -1: pl.ds(0, 4)}[dx]
            xd = {0: pl.ds(4, 8), 1: pl.ds(0, 4), -1: pl.ds(12, 4)}[dx]
            ys = {0: pl.ds(0, 16), 1: pl.ds(12, 4), -1: pl.ds(0, 4)}[dy]
            yd = {0: pl.ds(4, 16), 1: pl.ds(0, 4), -1: pl.ds(20, 4)}[dy]
            if dz == 0:
                push(group, s.at[:, xs, ys], r.at[:, xd, yd], d)
            else:
                push(group, p.at[:, ys], q.at[:, 0 if dz == 1 else 1, 1 - dx, yd], d)

    lane24 = iota((24, 128), 1)

    def assemble_one(get, q, f, out):
        for b, (start, rows) in enumerate(((0, range(4, 8)), (4, range(8)), (12, range(4)))):
            m = jnp.where(lane24 < 64, q[f, 0, b], q[f, 1, b])
            for n, xl in enumerate(rows):
                out[start + n] = jnp.where(lane24 >= 64, get(start + n), roll(m, 60 - 4 * xl, 1))

    fields = own_coefficients(1)
    for f, value in enumerate(fields):
        p1c[f] = pack_one(value)
    for f in range(2):
        value = (fields[2 * f] + roll(fields[2 * f + 1], 64, 1)).reshape(8, 16, 128)
        s1c[f] = value
        r1c[f, 4:12, 4:20, :] = value
    send_one(ONE_C, s1c, p1c, r1c, q1c, (1,))

    def pack_two(value):
        packed = value[0:8, :]
        for x in range(1, 4):
            packed = packed + roll(value[8 * x : 8 * x + 8, :], 32 * x, 1)
        return packed

    def send_two(group, s, r, reach):
        for d in COLUMNS:
            if distance(d) not in reach:
                continue
            target = r.at[1 - d[0], 1 if d[1] else 0, gz]
            if d[1] == 0:
                push(group, s, target, d)
            else:
                half = pl.ds(4, 4) if d[1] == 1 else pl.ds(0, 4)
                push(group, s.at[:, half], target.at[:, half], d)

    def assemble_two(get, out):
        for b in range(3):
            for t in range(2):
                tiles = [get(b, t, z) for z in range(4)]
                for x in range(4):
                    value = roll(tiles[0], -32 * x, 1)
                    for z in range(1, 4):
                        value = jnp.where((lane >> 5) == z, roll(tiles[z], 32 * (z - x), 1), value)
                    out[4 * b + x, 8 * t : 8 * t + 8, :] = value

    def sweep(t):
        momentum, step = WEIGHTS[t + 1]
        ends = land(t)
        packed = None
        for x in ORDER:
            c, total = around(t, x, ends)
            new = (1.0 + momentum - step) * c + step * (gain[x] + inv_s[x] * total)
            if t > 0:
                new = new - momentum * v[t - 1, 1 + x, 8:40, :]
            v[t + 1, 1 + x, 8:40, :] = new
            if t == 2:
                continue
            packed = pack_ends(packed, new, x)
            if x == 15:
                exchange_x(t + 1)
        if t < 2:
            send_z[t + 1] = packed
            exchange_yz(t + 1)

    sent(FACES)
    received(ROUND + 0)
    sweep(0)

    send_one(ONE_C, s1c, p1c, r1c, q1c, (2,))
    for f, value in enumerate(own_coefficients(2)):
        s2c[f] = pack_two(value)
    r2c[1, 0, gz] = s2c[...]
    halves_of = lambda value: jnp.where(sub < 4, value, roll(value, 64, 1))
    total = None
    for f, value in enumerate(own_coefficients(3)):
        halves = halves_of(value)
        halves = roll(halves + roll(halves, 4, 0), 16 * f, 1)
        total = halves if total is None else total + halves
    parity, chip = gy % 2, gy // 2
    r3[parity, chip, gx, gz] = total[0:4, :]
    block = r3.at[parity, chip, gx, gz]
    for d in (2, 1, 3):
        push(THREE_Z, block, block, (0, 0, d))

    sent(ROUND + 0)
    received(ROUND + 1)
    sweep(1)
    send_one(ONE_C, s1c, p1c, r1c, q1c, (3,))
    send_two(TWO_C, s2c, r2c, (1, 2, 3))

    def prepare(k, planes, scale):
        for x in range(planes):
            d = k[0, x]
            inverse = 1.0 / jnp.where(d > 0, d, 1.0)
            k[4, x] = inverse
            k[5, x] = scale * inverse
            k[6, x] = roll(k[2, x], -1, 0)
            k[7, x] = roll(k[3, x], -1, 1)

    received(THREE_Z)
    sent(THREE_Z)
    sent(ROUND + 1)
    received(ROUND + 2)
    sweep(2)

    for x in range(0, 16, 2):
        pair, ends = None, None
        for y in (x, x + 1):
            c, total = around(3, y, None)
            r = (src[y] - diag[y] * c) + total
            e = jnp.where(lane32 == 127, hz[y] * c, jnp.where(lane32 == 0, bz[y] * c, 0.0))
            pair = r if pair is None else pair + r
            ends = e if ends is None else ends + e
            fold[320 + y : 321 + y, :] = by[y, 0:1, :] * c[0:1, :]
            fold[336 + y : 337 + y, :] = hy[y, 31:32, :] * c[31:32, :]
        fold[16 * x : 16 * x + 32, :] = pair
        tmp[16 * x : 16 * x + 32, :] = ends
    fold[256:288, :] = bx[0] * v[3, 1, 8:40, :]
    fold[288:320, :] = bx[16] * v[3, 16, 8:40, :]
    value = fold[pl.ds(0, 176, stride=2), :] + fold[pl.ds(1, 176, stride=2), :]
    value = dot(value, picker("pair", 0, 64, 64)) * 0.125
    ends = (tmp[pl.ds(0, 128, stride=2), :] + tmp[pl.ds(1, 128, stride=2), :]) * 0.125
    lane128 = iota((128, 128), 1)
    ends = jnp.where(lane128 == 0, roll(ends, 1, 1), jnp.where(lane128 == 63, roll(ends, 63, 1), 0.0))
    own_block = value[0:128, :] + ends
    for x in range(8):
        s1s[1 + x, 4:20, :] = own_block[16 * x : 16 * x + 16, :]
        s1s[1 + x, 3:4, :] = value[160 + x : 161 + x, :]
        s1s[1 + x, 20:21, :] = value[168 + x : 169 + x, :]
    s1s[0, 4:20, :] = value[128:144, :]
    s1s[9, 4:20, :] = value[144:160, :]
    packed = jnp.zeros((24, 128), F32)
    for e in range(10):
        low_group = (lane24 >= 5 * e) & (lane24 < 5 * e + 5)
        high_group = (lane24 >= 5 * e + 67) & (lane24 < 5 * e + 72)
        packed = jnp.where(low_group | high_group, roll(s1s[e], 5 * e + 4, 1), packed)
    p1s[...] = packed
    for d in BOX:
        dx, dy, dz = d
        es = {0: pl.ds(0, 10), 1: pl.ds(5, 5), -1: pl.ds(0, 5)}[dx]
        ys = {0: pl.ds(0, 24), 1: pl.ds(16, 8), -1: pl.ds(0, 8)}[dy]
        yd = {0: pl.ds(0, 24), 1: pl.ds(24, 8), -1: pl.ds(32, 8)}[dy]
        if dz == 0:
            push(ONE_S, s1s.at[es, ys], r1s.at[1 - dx, es, yd], d)
        else:
            push(ONE_S, p1s.at[ys], q1s.at[0 if dz == 1 else 1, 1 - dx, yd], d)
    for e in range(10):
        r1s[1, e, 0:24, :] = s1s[e]

    send_two(TWO_C, s2c, r2c, (4,))
    block = r3.at[parity, chip, gx]
    for d in (4, 3, 5, 2, 6, 1, 7):
        push(THREE_X, block, block, (d, 0, 0))
    result = pltpu.make_async_copy(v.at[3, 1:17, 8:40], o0_h, out_sem)
    result.start()

    received(ONE_C)
    for f in range(4):
        if f % 2 == 0:
            assemble_one(lambda x, f=f: r1c[f // 2, x], q1c, f, k1.at[f])
        else:
            assemble_one(lambda x, f=f: roll(r1c[f // 2, x], 64, 1), q1c, f, k1.at[f])
    prepare(k1, 16, 0.25)
    sent(ONE_C)
    sent(ROUND + 2)
    received(ONE_S)

    def wide_around(k, c, lower, upper, x):
        total = k[1, x] * lower + k[1, x + 1] * upper
        total = total + (k[2, x] * roll(c, 1, 0) + k[6, x] * roll(c, -1, 0))
        return total + (k[3, x] * roll(c, 1, 1) + k[7, x] * roll(c, -1, 1))

    def wide_level(k, u, planes):
        for x in range(planes):
            g = k[4, x] * k[8, x]
            k[9, x] = g
            u[0, x] = WEIGHTS[0][1] * g
        for t in range(1, SWEEPS):
            momentum, step = WEIGHTS[t]
            for x in range(t, planes - t):
                c = u[t - 1, x]
                total = wide_around(k, c, u[t - 1, x - 1], u[t - 1, x + 1], x)
                new = (1.0 + momentum - step) * c + step * (k[9, x] + k[5, x] * total)
                if t > 1:
                    new = new - momentum * u[t - 2, x]
                u[t, x] = new

    def wide_residual(k, u, x, scale):
        c = u[3, x]
        total = wide_around(k, c, u[3, x - 1], u[3, x + 1], x)
        return (k[8, x] - k[0, x] * c) + scale * total

    def overlap(value):
        return jnp.concatenate(
            [value[0:8] + value[24:32], value[8:16], value[16:24] + value[32:40]], axis=0
        )

    middle_lanes = (lane24 >= 63) | (lane24 == 0)
    side_lanes = ((lane24 >= 60) & (lane24 <= 64)) | (lane24 <= 3) | (lane24 == 127)
    lane40 = iota((40, 128), 1)
    sides = [overlap(jnp.where(lane40 < 58, q1s[0, b], q1s[1, b])) for b in range(3)]
    for x in range(16):
        total = None
        for b, e in ((1, x - 3), (2, x - 11), (0, x + 5)):
            if not (5 if b == 0 else 0) <= e <= (4 if b == 2 else 9):
                continue
            part = jnp.where(middle_lanes, overlap(r1s[b, e]), 0.0)
            part = part + jnp.where(side_lanes, roll(sides[b], 60 - 5 * e, 1), 0.0)
            total = part if total is None else total + part
        k1[8, x] = total
    wide_level(k1, u1, 16)
    lane16 = iota((16, 128), 1)
    for x in range(4):
        r = wide_residual(k1, u1, 4 + 2 * x, 0.25) + wide_residual(k1, u1, 5 + 2 * x, 0.25)
        fold[16 * x : 16 * x + 16, :] = jnp.where(lane16 >= 64, r[4:20, :], 0.0)
    value = fold[pl.ds(0, 32, stride=2), :] + fold[pl.ds(1, 32, stride=2), :]
    value = dot(value, picker("pair", 64, 32, 0)) * 0.125
    s2s[0] = pack_two(value)
    r2s[1, 0, gz] = s2s[...]
    send_two(TWO_S, s2s, r2s, (1, 2, 3, 4))
    for x in range(8):
        o1[x] = roll(u1[3, 4 + x, 4:20, :], 64, 1)[:, 0:64]
    received(THREE_X)
    block = r3.at[parity, chip]
    for d in (4, 2, 6):
        push(THREE_Y, block, block, (0, d, 0))
    sent(THREE_X)
    sent(TWO_C)
    received(TWO_C)
    for f in range(4):
        assemble_two(lambda b, t, z, f=f: r2c[b, t, z, f], k2.at[f])
    prepare(k2, 12, 0.25**2)
    sent(ONE_S)
    received(TWO_S)

    assemble_two(lambda b, t, z: r2s[b, t, z, 0], k2.at[8])
    wide_level(k2, u2, 12)
    for x in range(2):
        r = wide_residual(k2, u2, 4 + 2 * x, 0.25**2) + wide_residual(k2, u2, 5 + 2 * x, 0.25**2)
        fold[8 * x : 8 * x + 8, :] = r[0:8, :]
    value = fold[pl.ds(0, 8, stride=2), :] + fold[pl.ds(1, 8, stride=2), :]
    value = dot(value, picker("pair", 0, 64, 0)) * 0.125
    halves = halves_of(value)
    s3s[...] = (halves + roll(halves, 4, 0))[0:4, :]
    r3s[gx, gy] = s3s[...]
    for d in PLANE:
        push(THREE_S, s3s, r3s.at[gx, gy], d)
    for x in range(4):
        o2[x] = roll(u2[3, 4 + x, 0:8, :], 128 - 32 * gz, 1)[:, 0:32]
    received(THREE_Y)
    block = r3.at[parity]
    push(THREE_CORE, block, block, None, (gx, gy + 1 - 2 * parity, gz))
    received(THREE_CORE)
    group = (lane >> 4) & 3
    for x in range(8):
        for p in range(4):
            tiles = [jnp.concatenate([r3[0, p, x, z], r3[1, p, x, z]], axis=0) for z in range(4)]
            for f in range(4):
                value = roll(tiles[0], -16 * f, 1)
                for z in range(1, 4):
                    value = jnp.where(group == z, roll(tiles[z], 16 * (z - f), 1), value)
                k3[f, x, 8 * p : 8 * p + 8, :] = value
    lane8 = iota((32, 128), 1)
    for x in range(8):
        inverse = 1.0 / k3[0, x]
        k3[4, x] = inverse
        k3[5, x] = 0.25**3 * inverse
        k3[6, x] = roll(k3[2, x], -1, 0)
        k3[7, x] = roll(k3[3, x], -1, 1)
        here, after = roll(k3[1, x], 64, 1), roll(k3[1, (x + 1) % 8], 64, 1)
        k3[10, x] = jnp.where(lane8 < 64, here, after)
    sent(TWO_S)
    sent(THREE_Y)
    sent(THREE_CORE)
    received(THREE_S)

    for y in range(8):
        k3[8, :, 4 * y : 4 * y + 4, :] = r3s[:, y]

    def whole_around(t, x):
        c = u3[t, x]
        turned = roll(c, 64, 1)
        lower = jnp.where(lane8 < 64, roll(u3[t, (x + 7) % 8], 64, 1), turned)
        upper = jnp.where(lane8 < 64, turned, roll(u3[t, (x + 1) % 8], 64, 1))
        total = k3[1, x] * lower + k3[10, x] * upper
        total = total + (k3[2, x] * roll(c, 1, 0) + k3[6, x] * roll(c, -1, 0))
        return c, total + (k3[3, x] * roll(c, 1, 1) + k3[7, x] * roll(c, -1, 1))

    for x in range(8):
        g = k3[4, x] * k3[8, x]
        k3[9, x] = g
        u3[0, x] = WEIGHTS[0][1] * g
    for t in range(1, SWEEPS):
        momentum, step = WEIGHTS[t]
        for x in range(8):
            c, total = whole_around(t - 1, x)
            new = (1.0 + momentum - step) * c + step * (k3[9, x] + k3[5, x] * total)
            if t > 1:
                new = new - momentum * u3[t - 2, x]
            u3[t, x] = new
    for x in range(8):
        c, total = whole_around(3, x)
        r = (k3[8, x] - k3[0, x] * c) + 0.25**3 * total
        fold[32 * x : 32 * x + 32, :] = r + roll(r, 64, 1)
        for y in range(8):
            x3[x, y, 0:4, :] = c[4 * y : 4 * y + 4, :]
    value = fold[pl.ds(0, 128, stride=2), :] + fold[pl.ds(1, 128, stride=2), :]
    value = dot(value, picker("pair", 0, 32, 0)) * 0.125
    o4[...] = value.reshape(8, 16, 128)[:, :, 0:32]
    mine = x3[gx, gy]
    for half in range(2):
        o3[half] = roll(mine, (128 - 64 * half) - 16 * gz, 1)[0:4, 0:16]
    sent(THREE_S)
    result.wait()


def hand_over(*refs):
    for k in range(5):
        refs[5 + k][...] = refs[k][...]


def body(*args):
    vm = lambda *shape: pltpu.VMEM(shape, F32)
    scratch = [
        vm(16, 32, 128), vm(16, 32, 128), vm(17, 32, 128), vm(16, 32, 128), vm(16, 32, 128),
        vm(16, 32, 128), vm(16, 32, 128), vm(16, 32, 128), vm(16, 32, 128), vm(16, 32, 128),
        vm(4, 18, 48, 128),
        vm(32, 128), vm(16, 128), vm(8, 128), vm(32, 128), vm(16, 128), vm(8, 128),
        vm(4, 2, 16, 128), vm(4, 2, 8, 128), vm(4, 2, 16, 128), vm(4, 8, 128),
        vm(256, 128), vm(352, 128),
        vm(2, 8, 16, 128), vm(4, 16, 128), vm(10, 24, 128), vm(24, 128),
        vm(2, 16, 24, 128), vm(4, 2, 3, 24, 128), vm(3, 10, 40, 128), vm(2, 3, 40, 128),
        vm(10, 16, 24, 128), vm(4, 16, 24, 128),
        vm(4, 8, 128), vm(1, 8, 128), vm(3, 2, 4, 4, 8, 128), vm(3, 2, 4, 1, 8, 128),
        vm(10, 12, 16, 128), vm(4, 12, 16, 128),
        vm(2, 4, 8, 4, 4, 128), vm(4, 128), vm(8, 8, 4, 128), vm(11, 8, 32, 128), vm(4, 8, 32, 128),
        vm(8, 8, 8, 128), vm(2048, 128),
        pltpu.SemaphoreType.DMA((5,)), pltpu.SemaphoreType.DMA,
        pltpu.SemaphoreType.DMA((GROUPS,)), pltpu.SemaphoreType.DMA((GROUPS,)),
    ]
    out = lambda *shape: jax.ShapeDtypeStruct(shape, F32)
    results = pl.pallas_call(
        kernel,
        out_shape=(out(16, 32, 128), out(8, 16, 64), out(4, 8, 32), out(2, 4, 16), out(8, 16, 32)),
        in_specs=[pl.BlockSpec(memory_space=pl.ANY)] * 5,
        out_specs=[pl.BlockSpec(memory_space=pl.ANY)] + [pl.BlockSpec(memory_space=pltpu.VMEM)] * 4,
        scratch_shapes=scratch,
        compiler_params=pltpu.CompilerParams(
            collective_id=0, has_side_effects=True, vmem_limit_bytes=63 * 2**20
        ),
    )(*args)
    return pl.pallas_call(
        hand_over,
        out_shape=tuple(out(*r.shape) for r in results),
        in_specs=[pl.BlockSpec(memory_space=pltpu.VMEM)] * 5,
        out_specs=[pl.BlockSpec(memory_space=pltpu.VMEM)] * 5,
    )(*results)


def solution(mesh):
    spec = P(*AXES)
    return jax.shard_map(
        body,
        mesh=mesh,
        in_specs=(spec,) * 5,
        out_specs=(spec, spec, spec, spec, P()),
        check_vma=False,
    )
```

```python
import itertools

import jax
import jax.numpy as jnp
from jax import lax
from jax.experimental import pallas as pl
from jax.experimental.pallas import tpu as pltpu
from jax.sharding import PartitionSpec as P

MESH = pl.DeviceIdType.MESH
AXES = ("gx", "gy", "gz")
SIZES = (8, 8, 4)
SWEEPS = 4
F32 = jnp.float32


def distance(d):
    return sum(min(s % n, -s % n) for s, n in zip(d, SIZES))


def farthest_first(xs, ys, zs):
    directions = [d for d in itertools.product(xs, ys, zs) if d != (0, 0, 0)]
    return tuple(sorted(directions, key=lambda d: -distance(d)))


BOX = farthest_first((-1, 0, 1), (-1, 0, 1), (-1, 0, 1))
COLUMNS = farthest_first((-1, 0, 1), (-1, 0, 1), (0, 1, 2, 3))
PLANE = farthest_first(range(8), range(8), (0,))
SIX = tuple(d for d in BOX if distance(d) == 1)

FACES, ROUND, ONE_C, ONE_S, TWO_C, TWO_S = 0, 1, 5, 6, 7, 8
THREE_X, THREE_Z, THREE_Y, THREE_CORE, THREE_S, ROUND_X, GROUPS = 9, 10, 11, 12, 13, 14, 18

FIELDS = (
    ("a", "pair", "pair", "pair"),
    ("bx", "even", "pair", "pair"),
    ("by", "pair", "even", "pair"),
    ("bz", "pair", "pair", "even"),
    ("hx", "odd", "pair", "pair"),
    ("hy", "pair", "odd", "pair"),
    ("hz", "pair", "pair", "odd"),
)


def chebyshev_weights(count):
    middle, spread = 1.125, 0.875
    sharpness = middle / spread
    weights = [(0.0, 1.0 / middle)]
    rho_prev = 1.0 / sharpness
    for _ in range(1, count):
        rho_next = 1.0 / (2.0 * sharpness - rho_prev)
        weights.append((rho_next * rho_prev, 2.0 * rho_next / spread))
        rho_prev = rho_next
    return weights


WEIGHTS = chebyshev_weights(SWEEPS)


def neighbour(d):
    return tuple(
        lax.rem(lax.axis_index(a) + ((s + n) % n), n) for a, s, n in zip(AXES, d, SIZES)
    )


def iota(shape, dim):
    return lax.broadcasted_iota(jnp.int32, shape, dim)


def roll(value, shift, axis):
    n = value.shape[axis]
    if isinstance(shift, int):
        shift %= n
        if shift == 0:
            return value
    return pltpu.roll(value, shift, axis)


def picker(mode, first, count, out):
    row = iota((128, 128), 0) - first
    col = iota((128, 128), 1) - out
    hit = (row >> 1) == col
    hit = hit & (col >= 0) & (col < count)
    if mode != "pair":
        hit = hit & ((row & 1) == (0 if mode == "even" else 1))
    return jnp.where(hit, 1.0, 0.0).astype(jnp.bfloat16)


def dot(value, matrix):
    high = value.astype(jnp.bfloat16)
    rest = value - high.astype(F32)
    middle = rest.astype(jnp.bfloat16)
    low = (rest - middle.astype(F32)).astype(jnp.bfloat16)
    parts = jnp.concatenate([high, middle, low], axis=1)
    return jnp.dot(parts, jnp.concatenate([matrix] * 3, axis=0), preferred_element_type=F32)


def x_pick(value, mode):
    n = value.shape[0]
    grouped = value.reshape((n // 2, 2) + value.shape[1:])
    if mode == "pair":
        return grouped[:, 0] + grouped[:, 1]
    return grouped[:, 0 if mode == "even" else 1]


def y_pick(tmp, value, mode):
    rows = value.shape[0]
    tmp[0:rows, :] = value
    if mode == "pair":
        return tmp[pl.ds(0, rows // 2, stride=2), :] + tmp[pl.ds(1, rows // 2, stride=2), :]
    return tmp[pl.ds(0 if mode == "even" else 1, rows // 2, stride=2), :]


def kernel(
    src_h, a_h, bx_h, by_h, bz_h,
    o0_h, o1, o2, o3, o4,
    src, a0, bx, by, bz, hy, hz, diag, inv_s, gain, v,
    send_fx, send_fy, send_fz, next_x, next_y, next_z,
    recv_y, recv_z, send_y, send_z,
    tmp, fold,
    s1c, p1c, s1s, p1s, r1c, q1c, r1s, q1s, k1, u1,
    s2c, s2s, r2c, r2s, k2, u2,
    r3, s3s, r3s, k3, u3, x3, gauge,
    in_sem, out_sem, send_sem, recv_sem,
):
    gx, gy, gz = (lax.axis_index(a) for a in AXES)
    rows = {}

    def push(group, source, target, d, device=None):
        n = 1
        for extent in target.shape[:-1]:
            n *= extent
        rows[group] = rows.get(group, 0) + n
        pltpu.make_async_remote_copy(
            src_ref=source,
            dst_ref=target,
            send_sem=send_sem.at[group],
            recv_sem=recv_sem.at[group],
            device_id=neighbour(d) if device is None else device,
            device_id_type=MESH,
        ).start()

    def wait(group, sem):
        measure = gauge.at[0 : rows[group]]
        pltpu.make_async_copy(measure, measure, sem.at[group]).wait()

    def received(group):
        wait(group, recv_sem)

    def sent(group):
        wait(group, send_sem)

    barrier = pltpu.get_barrier_semaphore()
    for d in ((1, 0, 0), (0, 1, 0), (0, 0, 1)):
        pl.semaphore_signal(barrier, inc=1, device_id=neighbour(d), device_id_type=MESH)

    loads = []
    for k, (h, m) in enumerate(
        ((bx_h, bx.at[0:16]), (by_h, by), (bz_h, bz), (a_h, a0), (src_h, src))
    ):
        copy = pltpu.make_async_copy(h, m, in_sem.at[k])
        copy.start()
        loads.append(copy)
    for copy in loads:
        copy.wait()

    lane = iota((8, 128), 1)
    sub = iota((8, 128), 0)
    lane32 = iota((32, 128), 1)
    inner_x = jnp.where(gx > 0, 1.0, 0.0).astype(F32)
    inner_y = jnp.where(gy > 0, 1.0, 0.0).astype(F32)
    inner_z = jnp.where(gz > 0, 1.0, 0.0).astype(F32)

    def pack_ends(packed, value, x):
        for j in range(4):
            at = 32 * j + 2 * x
            moved = roll(value[8 * j : 8 * j + 8, :], at + 1, 1)
            packed = moved if packed is None else jnp.where((lane >> 1) == (at >> 1), moved, packed)
        return packed

    def unpack_ends(ends, x):
        return jnp.concatenate([roll(ends, -(32 * j + 2 * x + 1), 1) for j in range(4)], axis=0)

    send_fx[...] = bx[0] * inner_x
    packed = None
    for x in range(16):
        send_fy[x : x + 1, :] = by[x, 0:1, :] * inner_y
        packed = pack_ends(packed, bz[x], x)
    send_fz[...] = packed * inner_z

    zeros = jnp.zeros((32, 128), F32)
    v[3, 0, 8:40, :] = zeros
    v[3, 17, 8:40, :] = zeros
    for x in range(16):
        v[3, 1 + x, 7:8, :] = zeros[0:1, :]
        v[3, 1 + x, 40:41, :] = zeros[0:1, :]
    for e in range(10):
        s1s[e] = zeros[0:24, :]

    SHAPES = {1: (16, 32), 2: (8, 16), 3: (4, 8)}
    LANES = {1: (0, 64, 64), 2: (64, 32, 0), 3: (0, 16, 0)}
    OWN = {1: {}, 2: {}, 3: {}}

    def coarsen(level, names, fine):
        first, count, out = LANES[level]
        n, m = SHAPES[level]
        size = n * m // 4
        groups = {"pair": [], "even": []}
        for k, (name, xm, ym, zm) in enumerate(FIELDS):
            if name not in names:
                continue
            value = y_pick(tmp, x_pick(fine(name), xm).reshape(n // 2 * m, 128), ym)
            if zm == "odd":
                value = roll(value, -1, 1)
            groups["pair" if zm == "pair" else "even"].append((k, name, value))
        for zm, members in groups.items():
            value = jnp.concatenate([part for _, _, part in members], axis=0)
            value = dot(value, picker(zm, first, count, out))
            for at, (k, name, _) in enumerate(members):
                part = value[at * size : (at + 1) * size, :]
                OWN[level][k] = part * (0.125 if name == "a" else 0.25)

    INDEX = {f[0]: k for k, f in enumerate(FIELDS)}

    def own(level):
        n, m = SHAPES[level + 1] if level < 3 else (2, 4)
        return lambda name: OWN[level][INDEX[name]].reshape(n, m, 128)

    fine = {"a": a0, "by": by, "bz": bz, "hy": hy, "hz": hz}

    def level_zero(name):
        if name == "bx":
            return bx[0:16]
        if name == "hx":
            return bx[1:17]
        return fine[name][...]

    low = ("a", "bx", "by", "bz")
    high = ("hx", "hy", "hz")

    coarsen(1, low, level_zero)
    coarsen(2, low, own(1))
    coarsen(3, low, own(2))

    pl.semaphore_wait(barrier, 3)

    push(FACES, send_fx, next_x, (-1, 0, 0))
    push(FACES, send_fy, next_y, (0, -1, 0))
    push(FACES, send_fz, next_z, (0, 0, -1))

    def swap_lanes(from_low, from_high):
        odd = (lane & 1) == 1
        return jnp.where(odd, roll(from_low, 1, 1), roll(from_high, -1, 1))

    ORDER = (0, 15) + tuple(range(1, 15))

    def exchange_x(t):
        push(ROUND_X + t, v.at[t, 1, 8:40], v.at[t, 17, 8:40], (-1, 0, 0))
        push(ROUND_X + t, v.at[t, 16, 8:40], v.at[t, 0, 8:40], (1, 0, 0))

    def exchange_yz(t):
        for x in range(16):
            send_y[t, 0, x : x + 1, :] = v[t, 1 + x, 8:9, :]
            send_y[t, 1, x : x + 1, :] = v[t, 1 + x, 39:40, :]
        push(ROUND + t, send_z.at[t], recv_z.at[t, 1], (0, 0, -1))
        push(ROUND + t, send_z.at[t], recv_z.at[t, 0], (0, 0, 1))
        push(ROUND + t, send_y.at[t, 0], recv_y.at[t, 1], (0, -1, 0))
        push(ROUND + t, send_y.at[t, 1], recv_y.at[t, 0], (0, 1, 0))

    def land(t):
        for x in range(16):
            v[t, 1 + x, 7:8, :] = recv_y[t, 0, x : x + 1, :]
            v[t, 1 + x, 40:41, :] = recv_y[t, 1, x : x + 1, :]
        return swap_lanes(recv_z[t, 0], recv_z[t, 1])

    def around(t, x, ends):
        c = v[t, 1 + x, 8:40, :]
        halo = 0.0 if ends is None else unpack_ends(ends, x)
        below = jnp.where(lane32 == 0, halo, roll(c, 1, 1))
        above = jnp.where(lane32 == 127, halo, roll(c, -1, 1))
        total = bx[x] * v[t, x, 8:40, :] + bx[x + 1] * v[t, x + 2, 8:40, :]
        total = total + (by[x] * v[t, 1 + x, 7:39, :] + hy[x] * v[t, 1 + x, 9:41, :])
        return c, total + (bz[x] * below + hz[x] * above)

    received(FACES)
    bx[16] = next_x[...]
    ends = roll(next_z[...], -1, 1)
    packed = None
    row32 = iota((32, 128), 0)
    for x in ORDER:
        b = by[x]
        up = jnp.where(row32 == 31, jnp.broadcast_to(next_y[x : x + 1, :], (32, 128)), roll(b, -1, 0))
        hy[x] = up
        total = (bx[x] + bx[x + 1]) + (b + up)
        b = bz[x]
        halo = jnp.concatenate([roll(ends, -(32 * j + 2 * x + 1), 1) for j in range(4)], axis=0)
        up = jnp.where(lane32 == 127, halo, roll(b, -1, 1))
        hz[x] = up
        total = a0[x] + (total + (b + up))
        diag[x] = total
        inverse = 1.0 / total
        inv_s[x] = inverse
        g = inverse * src[x]
        gain[x] = g
        g = g * WEIGHTS[0][1]
        v[0, 1 + x, 8:40, :] = g
        packed = pack_ends(packed, g, x)
        if x == 15:
            exchange_x(0)
    send_z[0] = packed
    exchange_yz(0)

    coarsen(1, high, level_zero)
    coarsen(2, high, own(1))
    coarsen(3, high, own(2))
    bx[0] = bx[0] * inner_x
    for x in range(16):
        by[x, 0:1, :] = by[x, 0:1, :] * inner_y
        bz[x] = jnp.where(lane32 == 0, bz[x] * inner_z, bz[x])

    def own_coefficients(level):
        scale = 0.25**level
        get = OWN[level]
        a, lx, ly, lz, ux, uy, uz = (get[k] for k in range(7))
        d = a + scale * ((lx + ux) + (ly + uy) + (lz + uz))
        rows = d.shape[0]
        row = iota((rows, 128), 0)
        m = SHAPES[level][1] // 2
        first = LANES[level][2]
        lx = jnp.where(row < m, lx * inner_x, lx)
        ly = jnp.where((row & (m - 1)) == 0, ly * inner_y, ly)
        lz = jnp.where(iota((rows, 128), 1) == first, lz * inner_z, lz)
        return d, lx, ly, lz

    def pack_one(value):
        lane16 = iota((16, 128), 1) >> 2
        packed = None
        for x in range(8):
            moved = roll(value[16 * x : 16 * x + 16, :], 4 * x + 4, 1)
            if packed is None:
                packed = moved
            else:
                packed = jnp.where((lane16 == x) | (lane16 == x + 17), moved, packed)
        return packed

    def send_one(group, s, p, r, q, reach):
        for d in BOX:
            if distance(d) not in reach:
                continue
            dx, dy, dz = d
            xs = {0: pl.ds(0, 8), 1: pl.ds(4, 4), -1: pl.ds(0, 4)}[dx]
            xd = {0: pl.ds(4, 8), 1: pl.ds(0, 4), -1: pl.ds(12, 4)}[dx]
            ys = {0: pl.ds(0, 16), 1: pl.ds(12, 4), -1: pl.ds(0, 4)}[dy]
            yd = {0: pl.ds(4, 16), 1: pl.ds(0, 4), -1: pl.ds(20, 4)}[dy]
            if dz == 0:
                push(group, s.at[:, xs, ys], r.at[:, xd, yd], d)
            else:
                push(group, p.at[:, ys], q.at[:, 0 if dz == 1 else 1, 1 - dx, yd], d)

    lane24 = iota((24, 128), 1)

    def assemble_one(get, q, f, out):
        for b, (start, rows) in enumerate(((0, range(4, 8)), (4, range(8)), (12, range(4)))):
            m = jnp.where(lane24 < 64, q[f, 0, b], q[f, 1, b])
            for n, xl in enumerate(rows):
                out[start + n] = jnp.where(lane24 >= 64, get(start + n), roll(m, 60 - 4 * xl, 1))

    fields = own_coefficients(1)
    for f, value in enumerate(fields):
        p1c[f] = pack_one(value)
    for f in range(2):
        value = (fields[2 * f] + roll(fields[2 * f + 1], 64, 1)).reshape(8, 16, 128)
        s1c[f] = value
        r1c[f, 4:12, 4:20, :] = value
    send_one(ONE_C, s1c, p1c, r1c, q1c, (1,))

    def pack_two(value):
        packed = value[0:8, :]
        for x in range(1, 4):
            packed = packed + roll(value[8 * x : 8 * x + 8, :], 32 * x, 1)
        return packed

    def send_two(group, s, r, reach):
        for d in COLUMNS:
            if distance(d) not in reach:
                continue
            target = r.at[1 - d[0], 1 if d[1] else 0, gz]
            if d[1] == 0:
                push(group, s, target, d)
            else:
                half = pl.ds(4, 4) if d[1] == 1 else pl.ds(0, 4)
                push(group, s.at[:, half], target.at[:, half], d)

    def assemble_two(get, out):
        for b in range(3):
            for t in range(2):
                tiles = [get(b, t, z) for z in range(4)]
                for x in range(4):
                    value = roll(tiles[0], -32 * x, 1)
                    for z in range(1, 4):
                        value = jnp.where((lane >> 5) == z, roll(tiles[z], 32 * (z - x), 1), value)
                    out[4 * b + x, 8 * t : 8 * t + 8, :] = value

    def sweep(t):
        momentum, step = WEIGHTS[t + 1]
        received(ROUND + t)
        ends = land(t)
        packed = None
        for x in tuple(range(1, 15)) + (0, 15):
            if x == 0:
                received(ROUND_X + t)
            c, total = around(t, x, ends)
            new = (1.0 + momentum - step) * c + step * (gain[x] + inv_s[x] * total)
            if t > 0:
                new = new - momentum * v[t - 1, 1 + x, 8:40, :]
            v[t + 1, 1 + x, 8:40, :] = new
            if t == 2:
                continue
            packed = pack_ends(packed, new, x)
        if t < 2:
            exchange_x(t + 1)
            send_z[t + 1] = packed
            exchange_yz(t + 1)

    sent(FACES)
    sweep(0)

    send_one(ONE_C, s1c, p1c, r1c, q1c, (2,))
    for f, value in enumerate(own_coefficients(2)):
        s2c[f] = pack_two(value)
    r2c[1, 0, gz] = s2c[...]
    halves_of = lambda value: jnp.where(sub < 4, value, roll(value, 64, 1))
    total = None
    for f, value in enumerate(own_coefficients(3)):
        halves = halves_of(value)
        halves = roll(halves + roll(halves, 4, 0), 16 * f, 1)
        total = halves if total is None else total + halves
    parity, chip = gy % 2, gy // 2
    r3[parity, chip, gx, gz] = total[0:4, :]
    block = r3.at[parity, chip, gx, gz]
    for d in (2, 1, 3):
        push(THREE_Z, block, block, (0, 0, d))

    sent(ROUND + 0)
    sent(ROUND_X + 0)
    sweep(1)
    send_one(ONE_C, s1c, p1c, r1c, q1c, (3,))
    send_two(TWO_C, s2c, r2c, (1, 2, 3))

    def prepare(k, planes, scale):
        for x in range(planes):
            d = k[0, x]
            inverse = 1.0 / jnp.where(d > 0, d, 1.0)
            k[4, x] = inverse
            k[5, x] = scale * inverse
            k[6, x] = roll(k[2, x], -1, 0)
            k[7, x] = roll(k[3, x], -1, 1)

    received(THREE_Z)
    sent(THREE_Z)
    sent(ROUND + 1)
    sent(ROUND_X + 1)
    sweep(2)

    for x in range(0, 16, 2):
        pair, ends = None, None
        for y in (x, x + 1):
            c, total = around(3, y, None)
            r = (src[y] - diag[y] * c) + total
            e = jnp.where(lane32 == 127, hz[y] * c, jnp.where(lane32 == 0, bz[y] * c, 0.0))
            pair = r if pair is None else pair + r
            ends = e if ends is None else ends + e
            fold[320 + y : 321 + y, :] = by[y, 0:1, :] * c[0:1, :]
            fold[336 + y : 337 + y, :] = hy[y, 31:32, :] * c[31:32, :]
        fold[16 * x : 16 * x + 32, :] = pair
        tmp[16 * x : 16 * x + 32, :] = ends
    fold[256:288, :] = bx[0] * v[3, 1, 8:40, :]
    fold[288:320, :] = bx[16] * v[3, 16, 8:40, :]
    value = fold[pl.ds(0, 176, stride=2), :] + fold[pl.ds(1, 176, stride=2), :]
    value = dot(value, picker("pair", 0, 64, 64)) * 0.125
    ends = (tmp[pl.ds(0, 128, stride=2), :] + tmp[pl.ds(1, 128, stride=2), :]) * 0.125
    lane128 = iota((128, 128), 1)
    ends = jnp.where(lane128 == 0, roll(ends, 1, 1), jnp.where(lane128 == 63, roll(ends, 63, 1), 0.0))
    own_block = value[0:128, :] + ends
    for x in range(8):
        s1s[1 + x, 4:20, :] = own_block[16 * x : 16 * x + 16, :]
        s1s[1 + x, 3:4, :] = value[160 + x : 161 + x, :]
        s1s[1 + x, 20:21, :] = value[168 + x : 169 + x, :]
    s1s[0, 4:20, :] = value[128:144, :]
    s1s[9, 4:20, :] = value[144:160, :]
    packed = jnp.zeros((24, 128), F32)
    for e in range(10):
        low_group = (lane24 >= 5 * e) & (lane24 < 5 * e + 5)
        high_group = (lane24 >= 5 * e + 67) & (lane24 < 5 * e + 72)
        packed = jnp.where(low_group | high_group, roll(s1s[e], 5 * e + 4, 1), packed)
    p1s[...] = packed
    for d in BOX:
        dx, dy, dz = d
        es = {0: pl.ds(0, 10), 1: pl.ds(5, 5), -1: pl.ds(0, 5)}[dx]
        ys = {0: pl.ds(0, 24), 1: pl.ds(16, 8), -1: pl.ds(0, 8)}[dy]
        yd = {0: pl.ds(0, 24), 1: pl.ds(24, 8), -1: pl.ds(32, 8)}[dy]
        if dz == 0:
            push(ONE_S, s1s.at[es, ys], r1s.at[1 - dx, es, yd], d)
        else:
            push(ONE_S, p1s.at[ys], q1s.at[0 if dz == 1 else 1, 1 - dx, yd], d)
    for e in range(10):
        r1s[1, e, 0:24, :] = s1s[e]

    send_two(TWO_C, s2c, r2c, (4,))
    block = r3.at[parity, chip, gx]
    for d in (4, 3, 5, 2, 6, 1, 7):
        push(THREE_X, block, block, (d, 0, 0))
    result = pltpu.make_async_copy(v.at[3, 1:17, 8:40], o0_h, out_sem)
    result.start()

    received(ONE_C)
    for f in range(4):
        if f % 2 == 0:
            assemble_one(lambda x, f=f: r1c[f // 2, x], q1c, f, k1.at[f])
        else:
            assemble_one(lambda x, f=f: roll(r1c[f // 2, x], 64, 1), q1c, f, k1.at[f])
    prepare(k1, 16, 0.25)
    sent(ONE_C)
    sent(ROUND + 2)
    sent(ROUND_X + 2)
    received(ONE_S)

    def wide_around(k, c, lower, upper, x):
        total = k[1, x] * lower + k[1, x + 1] * upper
        total = total + (k[2, x] * roll(c, 1, 0) + k[6, x] * roll(c, -1, 0))
        return total + (k[3, x] * roll(c, 1, 1) + k[7, x] * roll(c, -1, 1))

    def wide_level(k, u, planes):
        for x in range(planes):
            g = k[4, x] * k[8, x]
            k[9, x] = g
            u[0, x] = WEIGHTS[0][1] * g
        for t in range(1, SWEEPS):
            momentum, step = WEIGHTS[t]
            for x in range(t, planes - t):
                c = u[t - 1, x]
                total = wide_around(k, c, u[t - 1, x - 1], u[t - 1, x + 1], x)
                new = (1.0 + momentum - step) * c + step * (k[9, x] + k[5, x] * total)
                if t > 1:
                    new = new - momentum * u[t - 2, x]
                u[t, x] = new

    def wide_residual(k, u, x, scale):
        c = u[3, x]
        total = wide_around(k, c, u[3, x - 1], u[3, x + 1], x)
        return (k[8, x] - k[0, x] * c) + scale * total

    def overlap(value):
        return jnp.concatenate(
            [value[0:8] + value[24:32], value[8:16], value[16:24] + value[32:40]], axis=0
        )

    middle_lanes = (lane24 >= 63) | (lane24 == 0)
    side_lanes = ((lane24 >= 60) & (lane24 <= 64)) | (lane24 <= 3) | (lane24 == 127)
    lane40 = iota((40, 128), 1)
    sides = [overlap(jnp.where(lane40 < 58, q1s[0, b], q1s[1, b])) for b in range(3)]
    for x in range(16):
        total = None
        for b, e in ((1, x - 3), (2, x - 11), (0, x + 5)):
            if not (5 if b == 0 else 0) <= e <= (4 if b == 2 else 9):
                continue
            part = jnp.where(middle_lanes, overlap(r1s[b, e]), 0.0)
            part = part + jnp.where(side_lanes, roll(sides[b], 60 - 5 * e, 1), 0.0)
            total = part if total is None else total + part
        k1[8, x] = total
    wide_level(k1, u1, 16)
    lane16 = iota((16, 128), 1)
    for x in range(4):
        r = wide_residual(k1, u1, 4 + 2 * x, 0.25) + wide_residual(k1, u1, 5 + 2 * x, 0.25)
        fold[16 * x : 16 * x + 16, :] = jnp.where(lane16 >= 64, r[4:20, :], 0.0)
    value = fold[pl.ds(0, 32, stride=2), :] + fold[pl.ds(1, 32, stride=2), :]
    value = dot(value, picker("pair", 64, 32, 0)) * 0.125
    s2s[0] = pack_two(value)
    r2s[1, 0, gz] = s2s[...]
    send_two(TWO_S, s2s, r2s, (1, 2, 3, 4))
    for x in range(8):
        o1[x] = roll(u1[3, 4 + x, 4:20, :], 64, 1)[:, 0:64]
    received(THREE_X)
    block = r3.at[parity, chip]
    for d in (4, 2, 6):
        push(THREE_Y, block, block, (0, d, 0))
    sent(THREE_X)
    sent(TWO_C)
    received(TWO_C)
    for f in range(4):
        assemble_two(lambda b, t, z, f=f: r2c[b, t, z, f], k2.at[f])
    prepare(k2, 12, 0.25**2)
    sent(ONE_S)
    received(TWO_S)

    assemble_two(lambda b, t, z: r2s[b, t, z, 0], k2.at[8])
    wide_level(k2, u2, 12)
    for x in range(2):
        r = wide_residual(k2, u2, 4 + 2 * x, 0.25**2) + wide_residual(k2, u2, 5 + 2 * x, 0.25**2)
        fold[8 * x : 8 * x + 8, :] = r[0:8, :]
    value = fold[pl.ds(0, 8, stride=2), :] + fold[pl.ds(1, 8, stride=2), :]
    value = dot(value, picker("pair", 0, 64, 0)) * 0.125
    halves = halves_of(value)
    s3s[...] = (halves + roll(halves, 4, 0))[0:4, :]
    r3s[gx, gy] = s3s[...]
    for d in PLANE:
        push(THREE_S, s3s, r3s.at[gx, gy], d)
    for x in range(4):
        o2[x] = roll(u2[3, 4 + x, 0:8, :], 128 - 32 * gz, 1)[:, 0:32]
    received(THREE_Y)
    block = r3.at[parity]
    push(THREE_CORE, block, block, None, (gx, gy + 1 - 2 * parity, gz))
    received(THREE_CORE)
    group = (lane >> 4) & 3
    for x in range(8):
        for p in range(4):
            tiles = [jnp.concatenate([r3[0, p, x, z], r3[1, p, x, z]], axis=0) for z in range(4)]
            for f in range(4):
                value = roll(tiles[0], -16 * f, 1)
                for z in range(1, 4):
                    value = jnp.where(group == z, roll(tiles[z], 16 * (z - f), 1), value)
                k3[f, x, 8 * p : 8 * p + 8, :] = value
    lane8 = iota((32, 128), 1)
    for x in range(8):
        inverse = 1.0 / k3[0, x]
        k3[4, x] = inverse
        k3[5, x] = 0.25**3 * inverse
        k3[6, x] = roll(k3[2, x], -1, 0)
        k3[7, x] = roll(k3[3, x], -1, 1)
        here, after = roll(k3[1, x], 64, 1), roll(k3[1, (x + 1) % 8], 64, 1)
        k3[10, x] = jnp.where(lane8 < 64, here, after)
    sent(TWO_S)
    sent(THREE_Y)
    sent(THREE_CORE)
    received(THREE_S)

    for y in range(8):
        k3[8, :, 4 * y : 4 * y + 4, :] = r3s[:, y]

    def whole_around(t, x):
        c = u3[t, x]
        turned = roll(c, 64, 1)
        lower = jnp.where(lane8 < 64, roll(u3[t, (x + 7) % 8], 64, 1), turned)
        upper = jnp.where(lane8 < 64, turned, roll(u3[t, (x + 1) % 8], 64, 1))
        total = k3[1, x] * lower + k3[10, x] * upper
        total = total + (k3[2, x] * roll(c, 1, 0) + k3[6, x] * roll(c, -1, 0))
        return c, total + (k3[3, x] * roll(c, 1, 1) + k3[7, x] * roll(c, -1, 1))

    for x in range(8):
        g = k3[4, x] * k3[8, x]
        k3[9, x] = g
        u3[0, x] = WEIGHTS[0][1] * g
    for t in range(1, SWEEPS):
        momentum, step = WEIGHTS[t]
        for x in range(8):
            c, total = whole_around(t - 1, x)
            new = (1.0 + momentum - step) * c + step * (k3[9, x] + k3[5, x] * total)
            if t > 1:
                new = new - momentum * u3[t - 2, x]
            u3[t, x] = new
    for x in range(8):
        c, total = whole_around(3, x)
        r = (k3[8, x] - k3[0, x] * c) + 0.25**3 * total
        fold[32 * x : 32 * x + 32, :] = r + roll(r, 64, 1)
        for y in range(8):
            x3[x, y, 0:4, :] = c[4 * y : 4 * y + 4, :]
    value = fold[pl.ds(0, 128, stride=2), :] + fold[pl.ds(1, 128, stride=2), :]
    value = dot(value, picker("pair", 0, 32, 0)) * 0.125
    o4[...] = value.reshape(8, 16, 128)[:, :, 0:32]
    mine = x3[gx, gy]
    for half in range(2):
        o3[half] = roll(mine, (128 - 64 * half) - 16 * gz, 1)[0:4, 0:16]
    sent(THREE_S)
    result.wait()


def hand_over(*refs):
    for k in range(5):
        refs[5 + k][...] = refs[k][...]


def body(*args):
    vm = lambda *shape: pltpu.VMEM(shape, F32)
    scratch = [
        vm(16, 32, 128), vm(16, 32, 128), vm(17, 32, 128), vm(16, 32, 128), vm(16, 32, 128),
        vm(16, 32, 128), vm(16, 32, 128), vm(16, 32, 128), vm(16, 32, 128), vm(16, 32, 128),
        vm(4, 18, 48, 128),
        vm(32, 128), vm(16, 128), vm(8, 128), vm(32, 128), vm(16, 128), vm(8, 128),
        vm(4, 2, 16, 128), vm(4, 2, 8, 128), vm(4, 2, 16, 128), vm(4, 8, 128),
        vm(256, 128), vm(352, 128),
        vm(2, 8, 16, 128), vm(4, 16, 128), vm(10, 24, 128), vm(24, 128),
        vm(2, 16, 24, 128), vm(4, 2, 3, 24, 128), vm(3, 10, 40, 128), vm(2, 3, 40, 128),
        vm(10, 16, 24, 128), vm(4, 16, 24, 128),
        vm(4, 8, 128), vm(1, 8, 128), vm(3, 2, 4, 4, 8, 128), vm(3, 2, 4, 1, 8, 128),
        vm(10, 12, 16, 128), vm(4, 12, 16, 128),
        vm(2, 4, 8, 4, 4, 128), vm(4, 128), vm(8, 8, 4, 128), vm(11, 8, 32, 128), vm(4, 8, 32, 128),
        vm(8, 8, 8, 128), vm(2048, 128),
        pltpu.SemaphoreType.DMA((5,)), pltpu.SemaphoreType.DMA,
        pltpu.SemaphoreType.DMA((GROUPS,)), pltpu.SemaphoreType.DMA((GROUPS,)),
    ]
    out = lambda *shape: jax.ShapeDtypeStruct(shape, F32)
    results = pl.pallas_call(
        kernel,
        out_shape=(out(16, 32, 128), out(8, 16, 64), out(4, 8, 32), out(2, 4, 16), out(8, 16, 32)),
        in_specs=[pl.BlockSpec(memory_space=pl.ANY)] * 5,
        out_specs=[pl.BlockSpec(memory_space=pl.ANY)] + [pl.BlockSpec(memory_space=pltpu.VMEM)] * 4,
        scratch_shapes=scratch,
        compiler_params=pltpu.CompilerParams(
            collective_id=0, has_side_effects=True, vmem_limit_bytes=63 * 2**20
        ),
    )(*args)
    return pl.pallas_call(
        hand_over,
        out_shape=tuple(out(*r.shape) for r in results),
        in_specs=[pl.BlockSpec(memory_space=pltpu.VMEM)] * 5,
        out_specs=[pl.BlockSpec(memory_space=pltpu.VMEM)] * 5,
    )(*results)


def solution(mesh):
    spec = P(*AXES)
    return jax.shard_map(
        body,
        mesh=mesh,
        in_specs=(spec,) * 5,
        out_specs=(spec, spec, spec, spec, P()),
        check_vma=False,
    )
```
